256 devices in a mesh: view: 16 (over y, z_hi), row: 16 (over z_lo, x, core).
Axes of the slice: x: 4, y: 4, z: 8 (z_hi: 4, z_lo: 2; z = z_hi * 2 + z_lo), core: 2. Of those that a mesh axis runs over, the one named last changes fastest.
Arguments:
- stream_in: bfloat16 [16, 16, 128, 2048], P('view', 'row'), may hold values from -6 to 6
- query_in: bfloat16 [16, 16, 128, 2048], P('view', 'row'), may hold values from -240 to 240
- key_in: bfloat16 [16, 16, 128, 2048], P('view', 'row'), may hold values from -8 to 8
- value_in: bfloat16 [16, 16, 128, 2048], P('view', 'row'), may hold values from -6 to 6
- out_weight: bfloat16 [2048, 2048], P('view'), may hold values from -0.5 to 0.5
- norm_gain: float32 [2048], replicated, may hold values from 0.1 to 1.9
- up_weight: bfloat16 [2048, 4096], P(None, 'view'), may hold values from -0.125 to 0.125
- conv_taps: float32 [3, 3, 4096], P(None, None, 'view'), may hold values from -2 to 2
- down_weight: bfloat16 [4096, 2048], P('view'), may hold values from -0.1875 to 0.1875
Outputs:
- result: bfloat16 [16, 16, 128, 2048], P('view', 'row')
The draws below stay inside these ranges and needn't reach their ends.
All inputs are finite; a program needn't handle non-finite values.
Results may differ from the reference program's by a relative error of at most 0.025.
Values may be sent and summed in bfloat16 or wider, within the bound.
No kernel may reach another device: no remote copies, remote signals or barrier semaphores. Data moves between devices by JAX's collectives and lax.ppermute only.
A program may use at most 64 MiB of HBM per device.

```python
import math
import jax
import jax.numpy as jnp
from jax import lax

D = 2048
HD = 128
FF = 4096
W = 128
VIEWS = 16
H_ROWS = 16
N_VIEW = 16


def shared_keys(key):
    base = jax.random.normal(jax.random.fold_in(key, 11), (VIEWS, H_ROWS, W, D), jnp.float32)
    return jnp.clip(base * 1.6, -8.0, 8.0)


def draw_key_in(key, part):
    shared = shared_keys(key)
    return shared.astype(jnp.bfloat16)


def draw_query_in(key, part):
    key = jax.random.fold_in(key, 1)
    values = jnp.clip(jax.random.normal(key, (VIEWS, H_ROWS, W, D), jnp.float32) * 1.6, -8.0, 8.0)
    return values.astype(jnp.bfloat16)


def block_levels(rng, dims, cuts, least, largest):
    gain, own = 1.0, jax.random.fold_in(rng, 6)
    for axis_at, shards_of in cuts:
        heights = jnp.exp(jax.random.uniform(jax.random.fold_in(own, axis_at), (shards_of,), jnp.float32, least / len(cuts), largest / len(cuts)))
        gain = gain * jnp.repeat(heights, dims[axis_at] // shards_of).reshape([-1 if axis == axis_at else 1 for axis in range(len(dims))])
    return gain


def scatter_about(stream_key, extent, width, bound, split=(), held_as=jnp.bfloat16):
    entries = jax.random.normal(stream_key, extent, jnp.float32) * width
    if len(split) > 0:
        entries = block_levels(stream_key, extent, split, -0.22, 0.18) * entries
    return jnp.clip(entries, min=-bound, max=bound).astype(held_as)


def setup_inputs(seed: int = 0) -> dict:
    seeds = jax.random.split(jax.random.key(seed), 10)
    return {
        "stream_in": scatter_about(seeds[0], (VIEWS, H_ROWS, W, D), 1.0, 6.0, ((0, 16), (1, 16))),
        "query_in": draw_query_in(jax.random.fold_in(seeds[9], 71), 0),
        "key_in": draw_key_in(jax.random.fold_in(seeds[9], 71), 0),
        "value_in": scatter_about(seeds[3], (VIEWS, H_ROWS, W, D), 1.0, 6.0, ((0, 16), (1, 16))),
        "out_weight": scatter_about(seeds[4], (D, D), HD ** -0.5, 0.5, ((0, 16),)),
        "norm_gain": jnp.clip(1.0 + 0.18 * jax.random.normal(seeds[5], (D,), jnp.float32), 0.1, 1.9),
        "up_weight": scatter_about(seeds[6], (D, FF), D ** -0.5, 0.125, ((1, 16),)),
        "conv_taps": scatter_about(seeds[7], (3, 3, FF), 9 ** -0.5, 2.0, ((2, 16),), jnp.float32),
        "down_weight": scatter_about(seeds[8], (FF, D), (FF // 4) ** -0.5, 0.1875, ((0, 16),)),
    }


def reference(stream_in, query_in, key_in, value_in, out_weight, norm_gain, up_weight, conv_taps, down_weight):
    scaling = 1.0 / math.sqrt(HD)
    head_count = D // HD

    def one_row(row_index):

        def take_row(array):
            row_slice = lax.dynamic_index_in_dim(array, row_index, 1, keepdims=False)
            return row_slice.reshape(VIEWS * W, head_count, HD).astype(jnp.float32)
        query_rows = take_row(query_in)
        key_rows = take_row(key_in)
        value_rows = take_row(value_in)
        scores = jnp.einsum('qhd,khd->hqk', query_rows, key_rows) * scaling
        weights = jax.nn.softmax(scores, axis=-1).astype(jnp.bfloat16).astype(jnp.float32)
        attended = jnp.einsum('hqk,khd->qhd', weights, value_rows).astype(jnp.bfloat16)
        return attended.reshape(VIEWS, W, D)
    attended = lax.map(one_row, jnp.arange(H_ROWS, dtype=jnp.int32))
    attended = jnp.transpose(attended, (1, 0, 2, 3)).reshape(-1, D)
    token_count = attended.shape[0]
    group_size = D // N_VIEW

    def add_heads(running, group_index):
        col_part = lax.dynamic_slice_in_dim(attended, group_index * group_size, group_size, 1)
        row_part = lax.dynamic_slice_in_dim(out_weight, group_index * group_size, group_size, 0)
        partial_sum = jnp.dot(col_part, row_part, preferred_element_type=jnp.float32).astype(jnp.bfloat16)
        return (running + partial_sum.astype(jnp.float32), None)
    mixed, _ = lax.scan(add_heads, jnp.zeros((token_count, D), jnp.float32), jnp.arange(N_VIEW, dtype=jnp.int32))
    stream = stream_in.reshape(-1, D).astype(jnp.float32) + mixed
    normed = (stream * lax.rsqrt(lax.optimization_barrier(jnp.mean(stream * stream, axis=-1, keepdims=True)) + 1e-06) * norm_gain).astype(jnp.bfloat16)
    up_proj = jnp.dot(normed, up_weight, preferred_element_type=jnp.float32).astype(jnp.bfloat16)
    up_proj = up_proj.reshape(VIEWS, H_ROWS, W, FF)

    def one_view(view_up):
        padded = jnp.pad(view_up.astype(jnp.float32), ((1, 1), (1, 1), (0, 0)))
        conv_sum = jnp.zeros((H_ROWS, W, FF), jnp.float32)
        for offset_row in range(3):
            for offset_col in range(3):
                conv_sum = conv_sum + conv_taps[offset_row, offset_col] * padded[offset_row:offset_row + H_ROWS, offset_col:offset_col + W, :]
        return jax.nn.gelu(conv_sum).astype(jnp.bfloat16)
    activated = lax.map(one_view, up_proj).reshape(-1, FF)
    hidden_group = FF // N_VIEW

    def add_hidden(running, group_index):
        col_part = lax.dynamic_slice_in_dim(activated, group_index * hidden_group, hidden_group, 1)
        row_part = lax.dynamic_slice_in_dim(down_weight, group_index * hidden_group, hidden_group, 0)
        partial_sum = jnp.dot(col_part, row_part, preferred_element_type=jnp.float32).astype(jnp.bfloat16)
        return (running + partial_sum.astype(jnp.float32), None)
    feed, _ = lax.scan(add_hidden, jnp.zeros((token_count, D), jnp.float32), jnp.arange(N_VIEW, dtype=jnp.int32))
    result = (stream + feed).astype(jnp.bfloat16)
    return result.reshape(VIEWS, H_ROWS, W, D)
```

```python
import math

import jax
import jax.numpy as jnp
from jax import lax
from jax.sharding import Mesh, PartitionSpec as P

HD = 128
VIEW = ("y", "zh")
ROW = ("zl", "x", "core")
NEAR = ("x", "core")


def attend(query_all, key_all, value_all):
    key_count, head_size = query_all.shape
    block_size = math.gcd(512, key_count)
    scaling = 1.0 / math.sqrt(head_size)

    def one_block(query_block):
        scores = jnp.dot(query_block, key_all.T, preferred_element_type=jnp.float32) * scaling
        weights = jax.nn.softmax(scores, axis=-1).astype(jnp.bfloat16)
        return jnp.dot(weights, value_all, preferred_element_type=jnp.float32).astype(jnp.bfloat16)

    blocks = query_all.reshape(key_count // block_size, block_size, head_size)
    return lax.map(one_block, blocks).reshape(key_count, head_size)


def body(
    stream_in, query_in, key_in, value_in, out_weight, norm_gain, up_weight, conv_taps, down_weight
):
    _, _, cols, dim = stream_in.shape
    views = lax.axis_size(VIEW)
    near = lax.axis_size(NEAR)
    spot = lax.axis_index(NEAR)
    heads = dim // HD
    hidden = up_weight.shape[1] // near

    mix_cols = dim // near
    mix_slice = lax.dynamic_slice_in_dim(out_weight, spot * mix_cols, mix_cols, 1)
    mix_part = lax.all_gather(mix_slice, VIEW, axis=0, tiled=True)
    mix_full = lax.all_gather(mix_part, NEAR, axis=0, tiled=False)
    up_slice = lax.dynamic_slice_in_dim(up_weight, spot * hidden, hidden, 1).T
    down_slice = lax.dynamic_slice_in_dim(down_weight, spot * hidden, hidden, 0)
    pair = lax.all_gather(jnp.stack([up_slice, down_slice]), VIEW, axis=1, tiled=True)
    up_rows, down_rows = pair[0], pair[1]
    taps_slice = lax.dynamic_slice_in_dim(conv_taps, spot * hidden, hidden, 2)
    taps = lax.all_gather(taps_slice, VIEW, axis=2, tiled=True)

    def split_heads(array):
        return array.reshape(cols, heads, HD).transpose(1, 0, 2)

    packed = jnp.stack([split_heads(a) for a in (query_in, key_in, value_in)], axis=1)
    moved = lax.all_to_all(packed, VIEW, split_axis=0, concat_axis=0, tiled=True)
    attended = attend(*(moved[:, i].reshape(views * cols, HD) for i in range(3)))
    back = lax.all_to_all(
        attended.reshape(views, cols, HD), VIEW, split_axis=0, concat_axis=0, tiled=True
    )
    tokens = back.transpose(1, 0, 2).reshape(cols, dim)

    mixed = jnp.einsum("tk,nkc->tnc", tokens, mix_full, preferred_element_type=jnp.float32)
    stream = stream_in.reshape(cols, dim).astype(jnp.float32) + mixed.reshape(cols, dim)
    normed = (
        stream * lax.rsqrt(jnp.mean(stream * stream, axis=-1, keepdims=True) + 1e-06) * norm_gain
    ).astype(jnp.bfloat16)

    piece = lax.all_gather(normed, NEAR, axis=0, tiled=True)
    up_proj = lax.dot_general(
        piece, up_rows, (((1,), (1,)), ((), ())), preferred_element_type=jnp.float32
    ).astype(jnp.bfloat16)
    units = up_rows.shape[0]
    image = up_proj.reshape(near, cols, units)
    low = lax.axis_index("zl") == 0
    edge = jnp.where(low, image[near - 1], image[0])
    other = lax.ppermute(edge, "zl", [(0, 1), (1, 0)])
    blank = jnp.zeros_like(other)
    rimmed = jnp.concatenate(
        [jnp.where(low, blank, other)[None], image, jnp.where(low, other, blank)[None]], axis=0
    )
    padded = jnp.pad(rimmed.astype(jnp.float32), ((0, 0), (1, 1), (0, 0)))
    conv_sum = jnp.zeros((near, cols, units), jnp.float32)
    for a in range(3):
        for b in range(3):
            conv_sum = conv_sum + taps[a, b] * padded[a : a + near, b : b + cols, :]
    activated = jax.nn.gelu(conv_sum).astype(jnp.bfloat16)
    product = jnp.dot(
        activated.reshape(-1, units), down_rows, preferred_element_type=jnp.float32
    ).astype(jnp.bfloat16)
    feed = lax.psum_scatter(product, NEAR, scatter_dimension=0, tiled=True)
    result = (stream + feed.astype(jnp.float32)).astype(jnp.bfloat16)
    return result.reshape(stream_in.shape)


def solution(mesh):
    fine = Mesh(mesh.devices.reshape(4, 4, 2, 4, 2), ("y", "zh", "zl", "x", "core"))
    tokens = P(VIEW, ROW, None, None)
    return jax.shard_map(
        body,
        mesh=fine,
        in_specs=(
            tokens,
            tokens,
            tokens,
            tokens,
            P(VIEW, None),
            P(),
            P(None, VIEW),
            P(None, None, VIEW),
            P(VIEW, None),
        ),
        out_specs=tokens,
        check_vma=False,
    )
```

```python
import functools
import math

import jax
import jax.numpy as jnp
from jax import lax
from jax.experimental import pallas as pl
from jax.experimental.pallas import tpu as pltpu
from jax.sharding import Mesh, PartitionSpec as P

HD = 128
VIEW = ("y", "zh")
ROW = ("zl", "x", "core")
NEAR = ("x", "core")
F32 = jnp.float32
BF16 = jnp.bfloat16
BIG = 56 * 1024 * 1024


def cost(flops, bytes_accessed, transcendentals=0):
    return pl.CostEstimate(
        flops=int(flops), bytes_accessed=int(bytes_accessed), transcendentals=int(transcendentals)
    )


def pack_kernel(heads, cols, q_ref, k_ref, v_ref, taps_ref, out_ref, sems):
    copies = []
    for h in range(heads):
        for i, ref in enumerate((q_ref, k_ref, v_ref)):
            copies.append(
                pltpu.make_async_copy(
                    ref.at[:, pl.ds(h * HD, HD)],
                    out_ref.at[h, pl.ds(i * cols, cols), :],
                    sems.at[4 * h + i],
                )
            )
        copies.append(
            pltpu.make_async_copy(
                taps_ref, out_ref.at[h, pl.ds(3 * cols, taps_ref.shape[0]), :], sems.at[4 * h + 3]
            )
        )
    for copy in copies:
        copy.start()
    for copy in copies:
        copy.wait()


def pack(query, key, value, taps):
    cols, dim = query.shape
    heads = dim // HD
    hbm = pl.BlockSpec(memory_space=pl.ANY)
    return pl.pallas_call(
        functools.partial(pack_kernel, heads, cols),
        out_shape=jax.ShapeDtypeStruct((heads, 3 * cols + taps.shape[0], HD), BF16),
        in_specs=[hbm] * 4,
        out_specs=hbm,
        scratch_shapes=[pltpu.SemaphoreType.DMA((4 * heads,))],
        cost_estimate=cost(0, 4 * 3 * cols * dim),
        name="pack_heads",
    )(query, key, value, taps)


def attend_kernel(factor, spot_ref, q_ref, k_ref, v_ref, out_ref):
    views, cols, _ = q_ref.shape
    key = k_ref[...].reshape(-1, HD)
    value = v_ref[...].reshape(-1, HD)
    x_at, core_at = spot_ref[0], spot_ref[1]
    lane = lax.broadcasted_iota(jnp.int32, (cols, HD), 1)
    for i in range(views):
        scores = lax.dot_general(
            q_ref[i], key, (((1,), (1,)), ((), ())), preferred_element_type=F32
        )
        top = jnp.max(scores, axis=-1, keepdims=True)
        weights = jnp.exp2((scores - top) * factor)
        total = jnp.sum(weights, axis=-1, keepdims=True)
        mixed = jnp.dot(weights.astype(BF16), value, preferred_element_type=F32) / total
        mixed = pltpu.roll(mixed, lax.rem(HD - 32 * x_at, HD), 1)
        swapped = jnp.where(
            lane % 32 < 16, pltpu.roll(mixed, HD - 16, 1), pltpu.roll(mixed, 16, 1)
        )
        out_ref[i] = jnp.where(core_at == 0, mixed, swapped).astype(BF16)


def attend(moved, spot, cols, step_views=2):
    views = moved.shape[0]
    factor = math.log2(math.e) / math.sqrt(HD)
    tokens = views * cols
    return pl.pallas_call(
        functools.partial(attend_kernel, factor),
        out_shape=jax.ShapeDtypeStruct((views, cols, HD), BF16),
        grid_spec=pltpu.PrefetchScalarGridSpec(
            num_scalar_prefetch=1,
            grid=(views // step_views,),
            in_specs=[
                pl.BlockSpec((step_views, cols, HD), lambda i, s: (i, 0, 0)),
                pl.BlockSpec((views, cols, HD), lambda i, s: (0, 1, 0)),
                pl.BlockSpec((views, cols, HD), lambda i, s: (0, 2, 0)),
            ],
            out_specs=pl.BlockSpec((step_views, cols, HD), lambda i, s: (i, 0, 0)),
        ),
        compiler_params=pltpu.CompilerParams(vmem_limit_bytes=BIG),
        cost_estimate=cost(4 * tokens * tokens * HD, 8 * tokens * HD, tokens * tokens),
        name="attend",
    )(spot, moved, moved, moved)


def mix_kernel(back_ref, stream_ref, gain_ref, *refs):
    w_refs, stream_out, normed_out, acc = refs[:8], refs[8], refs[9], refs[10]
    step = pl.program_id(0)
    heads = back_ref.shape[0]

    @pl.when(step == 0)
    def _():
        acc[...] = stream_ref[...].astype(F32)

    left = jnp.concatenate([back_ref[h] for h in range(heads)], axis=1)
    right = jnp.concatenate([w[h] for h in range(heads) for w in w_refs], axis=0)
    acc[...] += jnp.dot(left, right, preferred_element_type=F32)

    @pl.when(step == pl.num_programs(0) - 1)
    def _():
        stream = acc[...]
        stream_out[...] = stream
        scale = lax.rsqrt(jnp.mean(stream * stream, axis=-1, keepdims=True) + 1e-06)
        normed_out[...] = (stream * scale * gain_ref[...]).astype(BF16)


def mix(back, stream_in, gain, pieces, step_heads=2):
    heads, cols, _ = back.shape
    dim = stream_in.shape[1]
    strip = pieces[0].shape[1]
    whole = pl.BlockSpec((cols, dim), lambda i: (0, 0))
    return pl.pallas_call(
        mix_kernel,
        out_shape=[
            jax.ShapeDtypeStruct((cols, dim), F32),
            jax.ShapeDtypeStruct((cols, dim), BF16),
        ],
        grid=(heads // step_heads,),
        in_specs=[
            pl.BlockSpec((step_heads, cols, HD), lambda i: (i, 0, 0)),
            whole,
            pl.BlockSpec((1, dim), lambda i: (0, 0)),
        ]
        + [pl.BlockSpec((step_heads, strip, dim), lambda i: (i, 0, 0))] * len(pieces),
        out_specs=[whole, whole],
        scratch_shapes=[pltpu.VMEM((cols, dim), F32)],
        compiler_params=pltpu.CompilerParams(vmem_limit_bytes=BIG),
        cost_estimate=cost(2 * cols * dim * dim, 2 * dim * dim + 8 * cols * dim),
        name="mix_norm",
    )(back, stream_in, gain.reshape(1, dim), *pieces)


def up_kernel(x_ref, w_ref, out_ref):
    weight = w_ref[...].reshape(-1, w_ref.shape[-1])
    out_ref[0] = lax.dot_general(
        x_ref[0], weight, (((1,), (1,)), ((), ())), preferred_element_type=F32
    ).astype(BF16)


def up(piece, pair):
    rows, cols, dim = piece.shape
    views, both, _ = pair.shape
    units = views * both // 2
    return pl.pallas_call(
        up_kernel,
        out_shape=jax.ShapeDtypeStruct((rows, cols, units), BF16),
        grid=(rows,),
        in_specs=[
            pl.BlockSpec((1, cols, dim), lambda i: (i, 0, 0)),
            pl.BlockSpec((views, both // 2, dim), lambda i: (0, 0, 0)),
        ],
        out_specs=pl.BlockSpec((1, cols, units), lambda i: (i, 0, 0)),
        compiler_params=pltpu.CompilerParams(vmem_limit_bytes=BIG),
        cost_estimate=cost(2 * rows * cols * dim * units, 2 * dim * (rows * cols + units)),
        name="up",
    )(piece, pair)


def conv_kernel(low_ref, above_ref, row_ref, below_ref, other_ref, taps_ref, w_ref, out_ref):
    step, last = pl.program_id(0), pl.num_programs(0) - 1
    low = low_ref[0]
    cols, units = row_ref.shape[1:]
    keep_above = jnp.where((step > 0) | (low == 0), 1.0, 0.0)
    keep_below = jnp.where((step < last) | (low == 1), 1.0, 0.0)
    col = lax.broadcasted_iota(jnp.int32, (cols, HD), 0)
    parts = []
    for u in range(0, units, HD):
        at = pl.ds(u, HD)
        other = other_ref[:, at].astype(F32)
        above = jnp.where(step == 0, other, above_ref[0, :, at].astype(F32)) * keep_above
        below = jnp.where(step == last, other, below_ref[0, :, at].astype(F32)) * keep_below
        row = row_ref[0, :, at].astype(F32)
        sums = []
        for b in range(3):
            sums.append(
                taps_ref[pl.ds(b, 1), at] * above
                + taps_ref[pl.ds(3 + b, 1), at] * row
                + taps_ref[pl.ds(6 + b, 1), at] * below
            )
        conv = (
            sums[1]
            + jnp.where(col == 0, 0.0, pltpu.roll(sums[0], 1, 0))
            + jnp.where(col == cols - 1, 0.0, pltpu.roll(sums[2], cols - 1, 0))
        )
        inner = math.sqrt(2.0 / math.pi) * (conv + 0.044715 * (conv * conv * conv))
        parts.append((0.5 * conv * (1.0 + jnp.tanh(inner))).astype(BF16))
    active = jnp.concatenate(parts, axis=1)
    weight = w_ref[...].reshape(-1, w_ref.shape[-1])
    out_ref[0] = jnp.dot(active, weight, preferred_element_type=F32).astype(BF16)


def conv_down(low, hidden, other, taps, pair):
    rows, cols, units = hidden.shape
    views, both, dim = pair.shape
    row = functools.partial(pl.BlockSpec, (1, cols, units))
    return pl.pallas_call(
        conv_kernel,
        out_shape=jax.ShapeDtypeStruct((rows, cols, dim), BF16),
        grid_spec=pltpu.PrefetchScalarGridSpec(
            num_scalar_prefetch=1,
            grid=(rows,),
            in_specs=[
                row(lambda i, s: (jnp.maximum(i - 1, 0), 0, 0)),
                row(lambda i, s: (i, 0, 0)),
                row(lambda i, s: (jnp.minimum(i + 1, rows - 1), 0, 0)),
                pl.BlockSpec((cols, units), lambda i, s: (0, 0)),
                pl.BlockSpec(taps.shape, lambda i, s: (0, 0)),
                pl.BlockSpec((views, both // 2, dim), lambda i, s: (0, 1, 0)),
            ],
            out_specs=pl.BlockSpec((1, cols, dim), lambda i, s: (i, 0, 0)),
        ),
        compiler_params=pltpu.CompilerParams(vmem_limit_bytes=BIG),
        cost_estimate=cost(2 * rows * cols * dim * units, 2 * dim * (rows * cols + units)),
        name="conv_gelu_down",
    )(low, hidden, hidden, hidden, other, taps, pair)


def shift(array, axis, by):
    count = lax.axis_size(axis)
    return lax.ppermute(array, axis, [(i, (i + by) % count) for i in range(count)])


def body(
    stream_in, query_in, key_in, value_in, out_weight, norm_gain, up_weight, conv_taps, down_weight
):
    shape = stream_in.shape
    _, _, cols, dim = shape
    views = lax.axis_size(VIEW)
    near = lax.axis_size(NEAR)
    spot = lax.axis_index(NEAR)
    x_at, core_at = lax.axis_index("x"), lax.axis_index("core")
    part = up_weight.shape[1] // near
    flat = [a.reshape(cols, dim) for a in (stream_in, query_in, key_in, value_in)]

    own_taps = lax.dynamic_slice_in_dim(conv_taps, spot * part, part, 2).reshape(-1)
    high = lax.reduce_precision(own_taps, 8, 7)
    middle = lax.reduce_precision(own_taps - high, 8, 7)
    terms = jnp.concatenate([high, middle, own_taps - high - middle])
    term_rows = 8 * pl.cdiv(terms.size, 8 * HD)
    terms = jnp.pad(terms, (0, term_rows * HD - terms.size)).astype(BF16).reshape(term_rows, HD)

    packed = pack(*flat[1:], terms)
    moved = lax.all_to_all(packed, VIEW, split_axis=0, concat_axis=0, tiled=True)
    attended = attend(moved, jnp.stack([x_at, core_at]).astype(jnp.int32), cols)
    back = lax.all_to_all(attended, VIEW, split_axis=0, concat_axis=0, tiled=True)

    strip = out_weight.shape[0] // near
    mine = lax.dynamic_slice_in_dim(out_weight, spot * strip, strip, 0)
    mine = lax.all_gather(mine, VIEW, axis=0, tiled=False)
    up_slice = lax.dynamic_slice_in_dim(up_weight, spot * part, part, 1).T
    down_slice = lax.dynamic_slice_in_dim(down_weight, spot * part, part, 0)
    pair, mine = lax.optimization_barrier((jnp.concatenate([up_slice, down_slice]), mine))
    pair = lax.all_gather(pair, VIEW, axis=0, tiled=False)
    before, after = shift(mine, "x", 1), shift(mine, "x", -1)
    half = views // 2
    across = jnp.concatenate([shift(before[:half], "x", 1), shift(after[half:], "x", -1)])
    pieces = []
    for piece in (mine, after, across, before):
        pieces += [piece, shift(piece, "core", 1)]

    stream, normed = mix(back, flat[0], norm_gain, pieces)

    taps = moved[:, 3 * cols :].reshape(views, -1)[:, : 27 * part].astype(F32)
    taps = jnp.sum(taps.reshape(views, 3, 9, part), axis=1)
    taps = taps.transpose(1, 0, 2).reshape(9, views * part)
    piece = lax.all_gather(normed, NEAR, axis=0, tiled=False)
    hidden = up(piece, pair)
    low = lax.axis_index("zl")
    edge = jnp.where(low == 0, hidden[near - 1], hidden[0])
    other = shift(edge, "zl", 1)
    product = conv_down((1 - low).astype(jnp.int32).reshape(1), hidden, other, taps, pair)
    feed = lax.psum_scatter(product.reshape(-1, dim), NEAR, scatter_dimension=0, tiled=True)
    return (stream + feed.astype(F32)).astype(BF16).reshape(shape)


def solution(mesh):
    fine = Mesh(mesh.devices.reshape(4, 4, 2, 4, 2), ("y", "zh", "zl", "x", "core"))
    tokens = P(VIEW, ROW, None, None)
    return jax.shard_map(
        body,
        mesh=fine,
        in_specs=(
            tokens,
            tokens,
            tokens,
            tokens,
            P(VIEW, None),
            P(),
            P(None, VIEW),
            P(None, None, VIEW),
            P(VIEW, None),
        ),
        out_specs=tokens,
        check_vma=False,
    )
```

```python
import functools
import math

import jax
import jax.numpy as jnp
from jax import lax
from jax.experimental import pallas as pl
from jax.experimental.pallas import tpu as pltpu
from jax.sharding import Mesh, PartitionSpec as P

HD = 128
VIEW = ("y", "zh")
ROW = ("zl", "x", "core")
NEAR = ("x", "core")
F32 = jnp.float32
BF16 = jnp.bfloat16
BIG = 56 * 1024 * 1024


def cost(flops, bytes_accessed, transcendentals=0):
    return pl.CostEstimate(
        flops=int(flops), bytes_accessed=int(bytes_accessed), transcendentals=int(transcendentals)
    )


def pack_kernel(q_ref, k_ref, v_ref, taps_ref, out_ref):
    heads, cols = out_ref.shape[0], q_ref.shape[0]
    for h in range(heads):
        for i, ref in enumerate((q_ref, k_ref, v_ref)):
            out_ref[h, pl.ds(i * cols, cols), :] = ref[:, pl.ds(h * HD, HD)]
        out_ref[h, pl.ds(3 * cols, taps_ref.shape[0]), :] = taps_ref[...]


def pack(query, key, value, taps, steps=4):
    cols, dim = query.shape
    heads = dim // HD
    rows = 3 * cols + taps.shape[0]
    wide = pl.BlockSpec((cols, dim // steps), lambda i: (0, i))
    return pl.pallas_call(
        pack_kernel,
        out_shape=jax.ShapeDtypeStruct((heads, rows, HD), BF16),
        grid=(steps,),
        in_specs=[wide] * 3 + [pl.BlockSpec(taps.shape, lambda i: (0, 0))],
        out_specs=pl.BlockSpec((heads // steps, rows, HD), lambda i: (i, 0, 0)),
        cost_estimate=cost(0, 4 * 3 * cols * dim),
        name="pack_heads",
    )(query, key, value, taps)


def attend_kernel(factor, spot_ref, q_ref, k_ref, v_ref, out_ref):
    views, cols, _ = q_ref.shape
    key = k_ref[...].reshape(-1, HD)
    value = v_ref[...].reshape(-1, HD)
    x_at, core_at = spot_ref[0], spot_ref[1]
    lane = lax.broadcasted_iota(jnp.int32, (cols, HD), 1)
    for i in range(views):
        scores = lax.dot_general(
            q_ref[i], key, (((1,), (1,)), ((), ())), preferred_element_type=F32
        )
        top = jnp.max(scores, axis=-1, keepdims=True)
        weights = jnp.exp2((scores - top) * factor)
        total = jnp.sum(weights, axis=-1, keepdims=True)
        mixed = jnp.dot(weights.astype(BF16), value, preferred_element_type=F32) / total
        mixed = pltpu.roll(mixed, lax.rem(HD - 32 * x_at, HD), 1)
        swapped = jnp.where(
            lane % 32 < 16, pltpu.roll(mixed, HD - 16, 1), pltpu.roll(mixed, 16, 1)
        )
        out_ref[i] = jnp.where(core_at == 0, mixed, swapped).astype(BF16)


def attend(moved, spot, cols, step_views=2):
    views = moved.shape[0]
    factor = math.log2(math.e) / math.sqrt(HD)
    tokens = views * cols
    return pl.pallas_call(
        functools.partial(attend_kernel, factor),
        out_shape=jax.ShapeDtypeStruct((views, cols, HD), BF16),
        grid_spec=pltpu.PrefetchScalarGridSpec(
            num_scalar_prefetch=1,
            grid=(views // step_views,),
            in_specs=[
                pl.BlockSpec((step_views, cols, HD), lambda i, s: (i, 0, 0)),
                pl.BlockSpec((views, cols, HD), lambda i, s: (0, 1, 0)),
                pl.BlockSpec((views, cols, HD), lambda i, s: (0, 2, 0)),
            ],
            out_specs=pl.BlockSpec((step_views, cols, HD), lambda i, s: (i, 0, 0)),
        ),
        compiler_params=pltpu.CompilerParams(vmem_limit_bytes=BIG),
        cost_estimate=cost(4 * tokens * tokens * HD, 8 * tokens * HD, tokens * tokens),
        name="attend",
    )(spot, moved, moved, moved)


def mix_kernel(count, spot_ref, stream_ref, gain_ref, *refs):
    lefts, w_refs = refs[:count], refs[count:-3]
    stream_out, normed_out, acc = refs[-3:]
    step = pl.program_id(0)

    @pl.when(step == 0)
    def _():
        acc[...] = stream_ref[...].astype(F32)

    left = jnp.concatenate([ref[0] for ref in lefts], axis=1)
    right = jnp.concatenate([w[h] for h in range(count) for w in w_refs], axis=0)
    acc[...] += jnp.dot(left, right, preferred_element_type=F32)

    @pl.when(step == pl.num_programs(0) - 1)
    def _():
        stream = acc[...]
        stream_out[...] = stream
        scale = lax.rsqrt(jnp.mean(stream * stream, axis=-1, keepdims=True) + 1e-06)
        normed_out[...] = (stream * scale * gain_ref[...]).astype(BF16)


def mix(spot, back, stream_in, gain, pieces, count=2):
    heads, cols, _ = back.shape
    dim = stream_in.shape[1]
    strip = pieces[0].shape[1]
    whole = pl.BlockSpec((cols, dim), lambda i, s: (0, 0))

    def head_at(k):
        def index(i, s):
            j = i * count + k
            y = lax.rem(s[2] + j // 4, 4)
            zh = lax.rem(s[3] + j % 4, 4)
            return y * 4 + zh, 0, 0

        return pl.BlockSpec((1, cols, HD), index)

    return pl.pallas_call(
        functools.partial(mix_kernel, count),
        out_shape=[
            jax.ShapeDtypeStruct((cols, dim), F32),
            jax.ShapeDtypeStruct((cols, dim), BF16),
        ],
        grid_spec=pltpu.PrefetchScalarGridSpec(
            num_scalar_prefetch=1,
            grid=(heads // count,),
            in_specs=[whole, pl.BlockSpec((1, dim), lambda i, s: (0, 0))]
            + [head_at(k) for k in range(count)]
            + [pl.BlockSpec((count, strip, dim), lambda i, s: (i, 0, 0))] * len(pieces),
            out_specs=[whole, whole],
            scratch_shapes=[pltpu.VMEM((cols, dim), F32)],
        ),
        compiler_params=pltpu.CompilerParams(vmem_limit_bytes=BIG),
        cost_estimate=cost(2 * cols * dim * dim, 2 * dim * dim + 8 * cols * dim),
        name="mix_norm",
    )(spot, stream_in, gain.reshape(1, dim), *([back] * count), *pieces)


def up_kernel(spot_ref, same_ref, other_ref, w_ref, out_ref):
    cols, dim = same_ref.shape
    first = spot_ref[1] == 0
    same, other = same_ref[...], other_ref[...]
    rows = jnp.concatenate([jnp.where(first, same, other), jnp.where(first, other, same)])
    out = lax.dot_general(rows, w_ref[...], (((1,), (1,)), ((), ())), preferred_element_type=F32)
    out_ref[...] = out.astype(BF16).reshape(out_ref.shape)


def up(spot, same, other, weight):
    cols, dim = same.shape
    units = weight.shape[0]
    vmem = pl.BlockSpec(memory_space=pltpu.VMEM)
    return pl.pallas_call(
        up_kernel,
        out_shape=jax.ShapeDtypeStruct((2, cols, units), BF16),
        in_specs=[pl.BlockSpec(memory_space=pltpu.SMEM), vmem, vmem, vmem],
        out_specs=vmem,
        compiler_params=pltpu.CompilerParams(vmem_limit_bytes=BIG),
        cost_estimate=cost(4 * cols * dim * units, 2 * dim * (2 * cols + units)),
        name="up",
    )(spot, same, other, weight)


def conv_kernel(
    offset, spot_ref, above_ref, pair_ref, below_ref, edge_ref, taps_ref, w_ref, give_ref, keep_ref
):
    cols, units = edge_ref.shape
    x_at = lax.rem(spot_ref[0] + offset, 4)
    first_x, last_x = x_at == 0, x_at == 3
    core_at, low = spot_ref[1], spot_ref[4]
    keep_above = jnp.where(first_x & (low == 1), 0.0, 1.0)
    keep_below = jnp.where(last_x & (low == 0), 0.0, 1.0)
    col = lax.broadcasted_iota(jnp.int32, (cols, HD), 0)
    parts = [[], []]
    for u in range(0, units, HD):
        at = pl.ds(u, HD)
        edge = edge_ref[:, at].astype(F32)
        rows = [
            jnp.where(first_x, edge, above_ref[1, :, at].astype(F32)) * keep_above,
            pair_ref[0, :, at].astype(F32),
            pair_ref[1, :, at].astype(F32),
            jnp.where(last_x, edge, below_ref[0, :, at].astype(F32)) * keep_below,
        ]
        for r in range(2):
            sums = [
                taps_ref[pl.ds(b, 1), at] * rows[r]
                + taps_ref[pl.ds(3 + b, 1), at] * rows[r + 1]
                + taps_ref[pl.ds(6 + b, 1), at] * rows[r + 2]
                for b in range(3)
            ]
            conv = (
                sums[1]
                + jnp.where(col == 0, 0.0, pltpu.roll(sums[0], 1, 0))
                + jnp.where(col == cols - 1, 0.0, pltpu.roll(sums[2], cols - 1, 0))
            )
            inner = math.sqrt(2.0 / math.pi) * (conv + 0.044715 * (conv * conv * conv))
            parts[r].append((0.5 * conv * (1.0 + jnp.tanh(inner))).astype(BF16))
    active = jnp.concatenate([jnp.concatenate(p, axis=1) for p in parts], axis=0)
    out = jnp.dot(active, w_ref[...], preferred_element_type=F32)
    top, bottom = out[:cols].astype(BF16), out[cols:].astype(BF16)
    keep_ref[...] = jnp.where(core_at == 0, top, bottom)
    give_ref[...] = jnp.where(core_at == 0, bottom, top)


def conv_down(spot, offset, hidden, edge, taps, weight):
    _, cols, units = hidden[0].shape
    dim = weight.shape[1]
    vmem = pl.BlockSpec(memory_space=pltpu.VMEM)
    shape = jax.ShapeDtypeStruct((cols, dim), BF16)
    return pl.pallas_call(
        functools.partial(conv_kernel, offset),
        out_shape=[shape, shape],
        in_specs=[pl.BlockSpec(memory_space=pltpu.SMEM)] + [vmem] * 6,
        out_specs=[vmem, vmem],
        compiler_params=pltpu.CompilerParams(vmem_limit_bytes=BIG),
        cost_estimate=cost(4 * cols * dim * units, 2 * dim * (2 * cols + units)),
        name="conv_gelu_down",
    )(
        spot,
        hidden[(offset - 1) % 4],
        hidden[offset],
        hidden[(offset + 1) % 4],
        edge,
        taps,
        weight,
    )


def shift(array, axis, by):
    count = lax.axis_size(axis)
    return lax.ppermute(array, axis, [(i, (i + by) % count) for i in range(count)])


def gather4(array, axis):
    return [array, shift(array, axis, -1), shift(array, axis, 2), shift(array, axis, 1)]


def body(
    stream_in, query_in, key_in, value_in, out_weight, norm_gain, up_weight, conv_taps, down_weight
):
    shape = stream_in.shape
    _, _, cols, dim = shape
    views = lax.axis_size(VIEW)
    near = lax.axis_size(NEAR)
    at = lax.axis_index(NEAR)
    part = up_weight.shape[1] // near
    low = 1 - lax.axis_index("zl")
    spot = jnp.stack(
        [lax.axis_index(name) for name in ("x", "core", "y", "zh")] + [low]
    ).astype(jnp.int32)
    flat = [a.reshape(cols, dim) for a in (stream_in, query_in, key_in, value_in)]

    own_taps = lax.dynamic_slice_in_dim(conv_taps, at * part, part, 2).reshape(-1)
    high = lax.reduce_precision(own_taps, 8, 7)
    middle = lax.reduce_precision(own_taps - high, 8, 7)
    terms = jnp.concatenate([high, middle, own_taps - high - middle])
    term_rows = 8 * pl.cdiv(terms.size, 8 * HD)
    terms = jnp.pad(terms, (0, term_rows * HD - terms.size)).astype(BF16).reshape(term_rows, HD)

    packed = pack(*flat[1:], terms)
    moved = lax.all_to_all(packed, VIEW, split_axis=0, concat_axis=0, tiled=True)
    attended = attend(moved, spot, cols)
    back = lax.all_to_all(attended, VIEW, split_axis=0, concat_axis=0, tiled=True)

    strip = out_weight.shape[0] // near
    mine = lax.dynamic_slice_in_dim(out_weight, at * strip, strip, 0)
    up_slice = lax.dynamic_slice_in_dim(up_weight, at * part, part, 1).T
    down_slice = lax.dynamic_slice_in_dim(down_weight, at * part, part, 0)
    mine, up_slice, down_slice, _ = lax.optimization_barrier(
        (mine, up_slice, down_slice, packed)
    )
    mine = jnp.stack(gather4(mine, "zh"))
    mine = jnp.concatenate(gather4(mine, "y"))
    up_slice, mine = lax.optimization_barrier((up_slice, mine))
    before, after = shift(mine, "x", 1), shift(mine, "x", -1)
    half = views // 2
    across = jnp.concatenate([shift(before[:half], "x", 1), shift(after[half:], "x", -1)])
    pieces = []
    for piece in (mine, after, across, before):
        pieces += [piece, shift(piece, "core", 1)]

    up_rows = jnp.concatenate(gather4(jnp.concatenate(gather4(up_slice, "zh")), "y"))
    down_slice, _ = lax.optimization_barrier((down_slice, up_rows))
    down_rows = jnp.concatenate(gather4(jnp.concatenate(gather4(down_slice, "zh")), "y"))
    taps = moved[:, 3 * cols :].reshape(4, 4, -1)[:, :, : 27 * part].astype(F32)
    taps = jnp.sum(taps.reshape(4, 4, 3, 9, part), axis=2)
    for axis, name in enumerate(("y", "zh")):
        taps = lax.dynamic_slice_in_dim(
            jnp.concatenate([taps, taps], axis=axis), lax.axis_index(name), 4, axis
        )
    taps = taps.transpose(2, 0, 1, 3).reshape(9, views * part)

    stream, normed = mix(spot, back, flat[0], norm_gain, pieces)

    def both(row):
        return up(spot, row, shift(row, "core", 1), up_rows)

    half = cols // 2
    before, after = shift(normed, "x", 1), shift(normed, "x", -1)
    across = jnp.concatenate([shift(before[:half], "x", 1), shift(after[half:], "x", -1)])
    hidden = [both(row) for row in (normed, after, across, before)]
    edge = jnp.zeros_like(hidden[0][0])
    for offset in range(4):
        x_of = lax.rem(spot[0] + offset, 4)
        edge = jnp.where((low == 1) & (x_of == 3), hidden[offset][1], edge)
        edge = jnp.where((low == 0) & (x_of == 0), hidden[offset][0], edge)
    edge = shift(edge, "zl", 1)

    def reduced(offset):
        give, keep = conv_down(spot, offset, hidden, edge, taps, down_rows)
        return keep.astype(F32), shift(give, "core", 1).astype(F32)

    keep, got = reduced(2)
    total = (keep + got).astype(BF16)
    right, left = shift(total[:half], "x", 1), shift(total[half:], "x", -1)
    keep, got = reduced(1)
    right_late = shift((keep[half:] + got[half:]).astype(BF16), "x", 1)
    right = shift((keep[:half] + got[:half] + right.astype(F32)).astype(BF16), "x", 1)
    keep, got = reduced(3)
    left_late = shift((keep[:half] + got[:half]).astype(BF16), "x", -1)
    left = shift((keep[half:] + got[half:] + left.astype(F32)).astype(BF16), "x", -1)
    keep, got = reduced(0)
    result = stream + keep + got
    result = result + jnp.concatenate([right, right_late]).astype(F32)
    result = result + jnp.concatenate([left_late, left]).astype(F32)
    return result.astype(BF16).reshape(shape)


def solution(mesh):
    fine = Mesh(mesh.devices.reshape(4, 4, 2, 4, 2), ("y", "zh", "zl", "x", "core"))
    tokens = P(VIEW, ROW, None, None)
    return jax.shard_map(
        body,
        mesh=fine,
        in_specs=(
            tokens,
            tokens,
            tokens,
            tokens,
            P(VIEW, None),
            P(),
            P(None, VIEW),
            P(None, None, VIEW),
            P(VIEW, None),
        ),
        out_specs=tokens,
        check_vma=False,
    )
```

```python
import functools
import math

import jax
import jax.numpy as jnp
from jax import lax
from jax.experimental import pallas as pl
from jax.experimental.pallas import tpu as pltpu
from jax.sharding import Mesh, PartitionSpec as P

HD = 128
VIEW = ("y", "zh")
ROW = ("zl", "x", "core")
NEAR = ("x", "core")
F32 = jnp.float32
BF16 = jnp.bfloat16
BIG = 56 * 1024 * 1024


def cost(flops, bytes_accessed, transcendentals=0):
    return pl.CostEstimate(
        flops=int(flops), bytes_accessed=int(bytes_accessed), transcendentals=int(transcendentals)
    )


def pack_kernel(q_ref, k_ref, v_ref, out_ref):
    heads, cols = out_ref.shape[0], q_ref.shape[0]
    for h in range(heads):
        for i, ref in enumerate((q_ref, k_ref, v_ref)):
            out_ref[h, pl.ds(i * cols, cols), :] = ref[:, pl.ds(h * HD, HD)]


def pack(query, key, value, steps=4):
    cols, dim = query.shape
    heads = dim // HD
    wide = pl.BlockSpec((cols, dim // steps), lambda i: (0, i))
    return pl.pallas_call(
        pack_kernel,
        out_shape=jax.ShapeDtypeStruct((heads, 3 * cols, HD), BF16),
        grid=(steps,),
        in_specs=[wide] * 3,
        out_specs=pl.BlockSpec((heads // steps, 3 * cols, HD), lambda i: (i, 0, 0)),
        cost_estimate=cost(0, 4 * 3 * cols * dim),
        name="pack_heads",
    )(query, key, value)


def attend_kernel(factor, spot_ref, q_ref, k_ref, v_ref, out_ref):
    views, cols, _ = q_ref.shape
    key = k_ref[...].reshape(-1, HD)
    value = v_ref[...].reshape(-1, HD)
    x_at, core_at = spot_ref[0], spot_ref[1]
    lane = lax.broadcasted_iota(jnp.int32, (cols, HD), 1)
    for i in range(views):
        scores = lax.dot_general(
            q_ref[i], key, (((1,), (1,)), ((), ())), preferred_element_type=F32
        )
        top = jnp.max(scores, axis=-1, keepdims=True)
        weights = jnp.exp2((scores - top) * factor)
        total = jnp.sum(weights, axis=-1, keepdims=True)
        mixed = jnp.dot(weights.astype(BF16), value, preferred_element_type=F32) / total
        mixed = pltpu.roll(mixed, lax.rem(HD - 32 * x_at, HD), 1)
        swapped = jnp.where(
            lane % 32 < 16, pltpu.roll(mixed, HD - 16, 1), pltpu.roll(mixed, 16, 1)
        )
        out_ref[i] = jnp.where(core_at == 0, mixed, swapped).astype(BF16)


def attend(moved, spot, cols, step_views=2):
    views = moved.shape[0]
    factor = math.log2(math.e) / math.sqrt(HD)
    tokens = views * cols
    return pl.pallas_call(
        functools.partial(attend_kernel, factor),
        out_shape=jax.ShapeDtypeStruct((views, cols, HD), BF16),
        grid_spec=pltpu.PrefetchScalarGridSpec(
            num_scalar_prefetch=1,
            grid=(views // step_views,),
            in_specs=[
                pl.BlockSpec((step_views, cols, HD), lambda i, s: (i, 0, 0)),
                pl.BlockSpec((views, cols, HD), lambda i, s: (0, 1, 0)),
                pl.BlockSpec((views, cols, HD), lambda i, s: (0, 2, 0)),
            ],
            out_specs=pl.BlockSpec((step_views, cols, HD), lambda i, s: (i, 0, 0)),
        ),
        compiler_params=pltpu.CompilerParams(vmem_limit_bytes=BIG),
        cost_estimate=cost(4 * tokens * tokens * HD, 8 * tokens * HD, tokens * tokens),
        name="attend",
    )(spot, moved, moved, moved)


def mix_kernel(count, spot_ref, stream_ref, gain_ref, *refs):
    lefts, w_refs = refs[:count], refs[count:-3]
    stream_out, normed_out, acc = refs[-3:]
    step = pl.program_id(0)

    @pl.when(step == 0)
    def _():
        acc[...] = stream_ref[...].astype(F32)

    left = jnp.concatenate([ref[0] for ref in lefts], axis=1)
    right = jnp.concatenate([w[h] for h in range(count) for w in w_refs], axis=0)
    acc[...] += jnp.dot(left, right, preferred_element_type=F32)

    @pl.when(step == pl.num_programs(0) - 1)
    def _():
        stream = acc[...]
        stream_out[...] = stream
        scale = lax.rsqrt(jnp.mean(stream * stream, axis=-1, keepdims=True) + 1e-06)
        normed_out[...] = (stream * scale * gain_ref[...]).astype(BF16)


def mix(spot, back, stream_in, gain, pieces, count=2):
    heads, cols, _ = back.shape
    dim = stream_in.shape[1]
    strip = pieces[0].shape[1]
    whole = pl.BlockSpec((cols, dim), lambda i, s: (0, 0))

    def head_at(k):
        def index(i, s):
            j = i * count + k
            y = lax.rem(s[2] + j // 4, 4)
            zh = lax.rem(s[3] + j % 4, 4)
            return y * 4 + zh, 0, 0

        return pl.BlockSpec((1, cols, HD), index)

    return pl.pallas_call(
        functools.partial(mix_kernel, count),
        out_shape=[
            jax.ShapeDtypeStruct((cols, dim), F32),
            jax.ShapeDtypeStruct((cols, dim), BF16),
        ],
        grid_spec=pltpu.PrefetchScalarGridSpec(
            num_scalar_prefetch=1,
            grid=(heads // count,),
            in_specs=[whole, pl.BlockSpec((1, dim), lambda i, s: (0, 0))]
            + [head_at(k) for k in range(count)]
            + [pl.BlockSpec((count, strip, dim), lambda i, s: (i, 0, 0))] * len(pieces),
            out_specs=[whole, whole],
            scratch_shapes=[pltpu.VMEM((cols, dim), F32)],
        ),
        compiler_params=pltpu.CompilerParams(vmem_limit_bytes=BIG),
        cost_estimate=cost(2 * cols * dim * dim, 2 * dim * dim + 8 * cols * dim),
        name="mix_norm",
    )(spot, stream_in, gain.reshape(1, dim), *([back] * count), *pieces)


def up_kernel(spot_ref, same_ref, other_ref, w_ref, out_ref):
    cols, dim = same_ref.shape
    first = spot_ref[1] == 0
    same, other = same_ref[...], other_ref[...]
    rows = jnp.concatenate([jnp.where(first, same, other), jnp.where(first, other, same)])
    weight = w_ref[...].reshape(-1, dim)
    out = lax.dot_general(rows, weight, (((1,), (1,)), ((), ())), preferred_element_type=F32)
    out_ref[...] = out.astype(BF16).reshape(out_ref.shape)


def share(pair, part, index):
    views, _, dim = pair.shape
    return pl.BlockSpec((views, part, dim), lambda i: (0, index, 0))


def whole(array):
    return pl.BlockSpec(array.shape, lambda i: (0,) * len(array.shape))


def up(spot, same, other, pair, part):
    cols, dim = same.shape
    units = pair.shape[0] * part
    shape = jax.ShapeDtypeStruct((2, cols, units), BF16)
    return pl.pallas_call(
        up_kernel,
        out_shape=shape,
        grid=(1,),
        in_specs=[
            pl.BlockSpec(memory_space=pltpu.SMEM),
            whole(same),
            whole(other),
            share(pair, part, 0),
        ],
        out_specs=whole(shape),
        compiler_params=pltpu.CompilerParams(vmem_limit_bytes=BIG),
        cost_estimate=cost(4 * cols * dim * units, 2 * dim * (2 * cols + units)),
        name="up",
    )(spot, same, other, pair)


def conv_kernel(
    offset, spot_ref, above_ref, pair_ref, below_ref, edge_ref, taps_ref, w_ref, give_ref, keep_ref
):
    cols, units = edge_ref.shape
    x_at = lax.rem(spot_ref[0] + offset, 4)
    first_x, last_x = x_at == 0, x_at == 3
    core_at, low = spot_ref[1], spot_ref[4]
    keep_above = jnp.where(first_x & (low == 1), 0.0, 1.0)
    keep_below = jnp.where(last_x & (low == 0), 0.0, 1.0)
    col = lax.broadcasted_iota(jnp.int32, (cols, HD), 0)
    parts = [[], []]
    for u in range(0, units, HD):
        at = pl.ds(u, HD)
        edge = edge_ref[:, at].astype(F32)
        rows = [
            jnp.where(first_x, edge, above_ref[1, :, at].astype(F32)) * keep_above,
            pair_ref[0, :, at].astype(F32),
            pair_ref[1, :, at].astype(F32),
            jnp.where(last_x, edge, below_ref[0, :, at].astype(F32)) * keep_below,
        ]
        for r in range(2):
            sums = [
                taps_ref[pl.ds(b, 1), at] * rows[r]
                + taps_ref[pl.ds(3 + b, 1), at] * rows[r + 1]
                + taps_ref[pl.ds(6 + b, 1), at] * rows[r + 2]
                for b in range(3)
            ]
            conv = (
                sums[1]
                + jnp.where(col == 0, 0.0, pltpu.roll(sums[0], 1, 0))
                + jnp.where(col == cols - 1, 0.0, pltpu.roll(sums[2], cols - 1, 0))
            )
            inner = math.sqrt(2.0 / math.pi) * (conv + 0.044715 * (conv * conv * conv))
            parts[r].append((0.5 * conv * (1.0 + jnp.tanh(inner))).astype(BF16))
    active = jnp.concatenate([jnp.concatenate(p, axis=1) for p in parts], axis=0)
    weight = w_ref[...].reshape(-1, w_ref.shape[-1])
    out = jnp.dot(active, weight, preferred_element_type=F32)
    top, bottom = out[:cols].astype(BF16), out[cols:].astype(BF16)
    keep_ref[...] = jnp.where(core_at == 0, top, bottom)
    give_ref[...] = jnp.where(core_at == 0, bottom, top)


def conv_down(spot, offset, hidden, edge, taps, pair, part):
    _, cols, units = hidden[0].shape
    dim = pair.shape[2]
    shape = jax.ShapeDtypeStruct((cols, dim), BF16)
    near = [hidden[(offset + by) % 4] for by in (-1, 0, 1)]
    return pl.pallas_call(
        functools.partial(conv_kernel, offset),
        out_shape=[shape, shape],
        grid=(1,),
        in_specs=[pl.BlockSpec(memory_space=pltpu.SMEM)]
        + [whole(a) for a in (*near, edge, taps)]
        + [share(pair, part, 1)],
        out_specs=[whole(shape)] * 2,
        compiler_params=pltpu.CompilerParams(vmem_limit_bytes=BIG),
        cost_estimate=cost(4 * cols * dim * units, 2 * dim * (2 * cols + units)),
        name="conv_gelu_down",
    )(spot, *near, edge, taps, pair)


def shift(array, axis, by):
    count = lax.axis_size(axis)
    return lax.ppermute(array, axis, [(i, (i + by) % count) for i in range(count)])


def gather4(array, axis):
    return [array, shift(array, axis, -1), shift(array, axis, 2), shift(array, axis, 1)]


def body(
    stream_in, query_in, key_in, value_in, out_weight, norm_gain, up_weight, conv_taps, down_weight
):
    shape = stream_in.shape
    _, _, cols, dim = shape
    views = lax.axis_size(VIEW)
    near = lax.axis_size(NEAR)
    at = lax.axis_index(NEAR)
    part = up_weight.shape[1] // near
    low = 1 - lax.axis_index("zl")
    spot = jnp.stack(
        [lax.axis_index(name) for name in ("x", "core", "y", "zh")] + [low]
    ).astype(jnp.int32)
    flat = [a.reshape(cols, dim) for a in (stream_in, query_in, key_in, value_in)]

    strip = out_weight.shape[0] // near
    mine = lax.dynamic_slice_in_dim(out_weight, at * strip, strip, 0)
    mine = jnp.stack(gather4(mine, "zh"))

    packed, mine = lax.optimization_barrier((pack(*flat[1:]), mine))
    moved = lax.all_to_all(packed, VIEW, split_axis=0, concat_axis=0, tiled=True)

    mine = jnp.concatenate(gather4(mine, "y"))
    before, after = shift(mine, "x", 1), shift(mine, "x", -1)

    own_taps = lax.dynamic_slice_in_dim(conv_taps, at * part, part, 2).reshape(-1)
    high = lax.reduce_precision(own_taps, 8, 7)
    middle = lax.reduce_precision(own_taps - high, 8, 7)
    terms = jnp.concatenate([high, middle, own_taps - high - middle])
    terms = jnp.pad(terms, (0, 8 * dim - terms.size)).astype(BF16).reshape(8, dim)
    up_slice = lax.dynamic_slice_in_dim(up_weight, at * part, part, 1).T
    down_slice = lax.dynamic_slice_in_dim(down_weight, at * part, part, 0)
    pair = jnp.concatenate([up_slice, down_slice, terms])
    moved, pair, before, after = lax.optimization_barrier((moved, pair, before, after))
    pair = lax.all_gather(pair, VIEW, axis=0, tiled=False)
    half = views // 2
    across = jnp.concatenate([shift(before[:half], "x", 1), shift(after[half:], "x", -1)])

    attended = attend(moved, spot, cols)
    attended, mine, after, across, before = lax.optimization_barrier(
        (attended, mine, after, across, before)
    )
    back = lax.all_to_all(attended, VIEW, split_axis=0, concat_axis=0, tiled=True)
    pieces = []
    for piece in (mine, after, across, before):
        pieces += [piece, shift(piece, "core", 1)]

    stream, normed = mix(spot, back, flat[0], norm_gain, pieces)

    taps = pair[:, 2 * part :].reshape(views, -1)[:, : 27 * part].astype(F32)
    taps = jnp.sum(taps.reshape(views, 3, 9, part), axis=1)
    taps = taps.transpose(1, 0, 2).reshape(9, views * part)

    def both(row):
        return up(spot, row, shift(row, "core", 1), pair, part)

    half = cols // 2
    before, after = shift(normed, "x", 1), shift(normed, "x", -1)
    across = jnp.concatenate([shift(before[:half], "x", 1), shift(after[half:], "x", -1)])
    hidden = [both(row) for row in (normed, after, across, before)]
    edge = jnp.zeros_like(hidden[0][0])
    for offset in range(4):
        x_of = lax.rem(spot[0] + offset, 4)
        edge = jnp.where((low == 1) & (x_of == 3), hidden[offset][1], edge)
        edge = jnp.where((low == 0) & (x_of == 0), hidden[offset][0], edge)
    edge = shift(edge, "zl", 1)

    def reduced(offset, hidden):
        give, keep = conv_down(spot, offset, hidden, edge, taps, pair, part)
        return keep, shift(give, "core", 1)

    def add(*terms):
        return sum(term.astype(F32) for term in terms).astype(BF16)

    keep_2, got_2 = reduced(2, hidden)
    keep_1, got_1 = reduced(1, hidden)
    total = add(keep_2, got_2)
    total, hidden = lax.optimization_barrier((total, hidden))
    right, left = shift(total[:half], "x", 1), shift(total[half:], "x", -1)
    right_late = shift(add(keep_1[half:], got_1[half:]), "x", 1)
    keep_3, got_3 = reduced(3, hidden)
    right = add(keep_1[:half], got_1[:half], right)
    left_late = shift(add(keep_3[:half], got_3[:half]), "x", -1)
    left = add(keep_3[half:], got_3[half:], left)
    right, left, hidden = lax.optimization_barrier((right, left, hidden))
    right, left = shift(right, "x", 1), shift(left, "x", -1)
    keep, got = reduced(0, hidden)
    result = stream + keep.astype(F32) + got.astype(F32)
    result = result + jnp.concatenate([right, right_late]).astype(F32)
    result = result + jnp.concatenate([left_late, left]).astype(F32)
    return result.astype(BF16).reshape(shape)


def solution(mesh):
    fine = Mesh(mesh.devices.reshape(4, 4, 2, 4, 2), ("y", "zh", "zl", "x", "core"))
    tokens = P(VIEW, ROW, None, None)
    return jax.shard_map(
        body,
        mesh=fine,
        in_specs=(
            tokens,
            tokens,
            tokens,
            tokens,
            P(VIEW, None),
            P(),
            P(None, VIEW),
            P(None, None, VIEW),
            P(VIEW, None),
        ),
        out_specs=tokens,
        check_vma=False,
    )
```

```python
import functools
import math

import jax
import jax.numpy as jnp
from jax import lax
from jax.experimental import pallas as pl
from jax.experimental.pallas import tpu as pltpu
from jax.sharding import Mesh, PartitionSpec as P

HD = 128
VIEW = ("y", "zh")
ROW = ("zl", "x", "core")
NEAR = ("x", "core")
F32 = jnp.float32
BF16 = jnp.bfloat16
MIB = 1024 * 1024
VMEM = pl.BlockSpec(memory_space=pltpu.VMEM)
SMEM = pl.BlockSpec(memory_space=pltpu.SMEM)


def call(kernel, name, limit, out_shape, in_specs, args, hides=False, out_specs=None, scratch=()):
    return pl.pallas_call(
        kernel,
        out_shape=out_shape,
        in_specs=in_specs,
        out_specs=out_specs or jax.tree.map(lambda _: VMEM, out_shape),
        scratch_shapes=list(scratch),
        compiler_params=pltpu.CompilerParams(vmem_limit_bytes=limit * MIB),
        cost_estimate=pl.CostEstimate(
            flops=30_000_000_000 if hides else 1000, bytes_accessed=1000, transcendentals=0
        ),
        name=name,
    )(*args)


def pack_kernel(q_ref, k_ref, v_ref, out_ref):
    heads, cols = out_ref.shape[0], q_ref.shape[0]
    for h in range(heads):
        for i, ref in enumerate((q_ref, k_ref, v_ref)):
            out_ref[h, pl.ds(i * cols, cols), :] = ref[:, pl.ds(h * HD, HD)]


def pack(query, key, value):
    cols, dim = query.shape
    shape = jax.ShapeDtypeStruct((dim // HD, 3 * cols, HD), BF16)
    return call(pack_kernel, "pack_heads", 6, shape, [VMEM] * 3, (query, key, value))


def attend_kernel(factor, step, moved_ref, out_ref):
    views, cols, _ = out_ref.shape
    key = moved_ref[:, pl.ds(cols, cols), :].reshape(-1, HD)
    value = moved_ref[:, pl.ds(2 * cols, cols), :].reshape(-1, HD)
    for i in range(0, views, step):
        query = moved_ref[pl.ds(i, step), pl.ds(0, cols), :].reshape(-1, HD)
        scores = lax.dot_general(
            query, key, (((1,), (1,)), ((), ())), preferred_element_type=F32
        )
        top = jnp.max(scores, axis=-1, keepdims=True)
        weights = jnp.exp2((scores - top) * factor)
        total = jnp.sum(weights, axis=-1, keepdims=True)
        mixed = jnp.dot(weights.astype(BF16), value, preferred_element_type=F32) / total
        out_ref[pl.ds(i, step)] = mixed.astype(BF16).reshape(step, cols, HD)


def attend(moved, cols):
    factor = math.log2(math.e) / math.sqrt(HD)
    shape = jax.ShapeDtypeStruct((moved.shape[0], cols, HD), BF16)
    return call(
        functools.partial(attend_kernel, factor, 2), "attend", 24, shape, [VMEM], (moved,), True
    )


def join_kernel(back_ref, out_ref):
    for h in range(back_ref.shape[0]):
        out_ref[:, pl.ds(h * HD, HD)] = back_ref[h]


def join(back):
    heads, cols, size = back.shape
    shape = jax.ShapeDtypeStruct((cols, heads * size), BF16)
    return call(join_kernel, "join_heads", 4, shape, [VMEM], (back,), True)


def mix_kernel(spot_ref, left_ref, stream_ref, gain_ref, *refs):
    w_refs, (stream_out, normed_out, acc, sem) = refs[:-4], refs[-4:]
    width = w_refs[0].shape[2]
    left = left_ref[...]
    for i, w_ref in enumerate(w_refs):
        core_at = spot_ref[1] if i % 2 == 0 else 1 - spot_ref[1]
        block = 2 * lax.rem(spot_ref[0] + i // 2, 4) + core_at
        at = pl.ds(pl.multiple_of(block * width, width), width)
        weight = w_ref[...].reshape(-1, width)
        acc[:, at] = stream_ref[:, at].astype(F32) + jnp.dot(
            left, weight, preferred_element_type=F32
        )
    copy = pltpu.make_async_copy(acc, stream_out, sem)
    copy.start()
    stream = acc[...]
    scale = lax.rsqrt(jnp.mean(stream * stream, axis=-1, keepdims=True) + 1e-06)
    normed_out[...] = (stream * scale * gain_ref[...]).astype(BF16)
    copy.wait()


def mix(spot, left, stream_in, gain, pieces):
    shapes = [jax.ShapeDtypeStruct(stream_in.shape, t) for t in (F32, BF16)]
    args = (spot, left, stream_in, gain.reshape(1, -1), *pieces)
    return call(
        mix_kernel,
        "mix_norm",
        8,
        shapes,
        [SMEM] + [VMEM] * (len(args) - 1),
        args,
        out_specs=[pl.BlockSpec(memory_space=pl.ANY), VMEM],
        scratch=[pltpu.VMEM(stream_in.shape, F32), pltpu.SemaphoreType.DMA],
    )


def up_kernel(spot_ref, *refs):
    rows_refs, (w_ref, out_ref, edge_ref) = refs[:-3], refs[-3:]
    first, low = spot_ref[1] == 0, spot_ref[4]
    rows = []
    for same_ref, other_ref in zip(rows_refs[::2], rows_refs[1::2]):
        same, other = same_ref[...], other_ref[...]
        rows += [jnp.where(first, same, other), jnp.where(first, other, same)]
    out = lax.dot_general(
        jnp.concatenate(rows), w_ref[...], (((1,), (1,)), ((), ())), preferred_element_type=F32
    )
    out_ref[...] = out.astype(BF16).reshape(out_ref.shape)
    edge_ref[...] = out_ref[2 * lax.rem(4 - low - spot_ref[0], 4) + low]


def up(spot, rows, weight):
    cols, units = rows[0].shape[0], weight.shape[0]
    shapes = [
        jax.ShapeDtypeStruct((len(rows), cols, units), BF16),
        jax.ShapeDtypeStruct((cols, units), BF16),
    ]
    args = (spot, *rows, weight)
    return call(up_kernel, "up", 16, shapes, [SMEM] + [VMEM] * (len(args) - 1), args)


def conv_kernel(offsets, spot_ref, *refs):
    hidden_ref, edge_ref, taps_ref, w_ref, *outs = refs
    cols, units = edge_ref.shape
    core_at, low = spot_ref[1], spot_ref[4]
    col = lax.broadcasted_iota(jnp.int32, (cols, HD), 0)
    for n, offset in enumerate(offsets):
        x_at = lax.rem(spot_ref[0] + offset, 4)
        first_x, last_x = x_at == 0, x_at == 3
        keep_above = jnp.where(first_x & (low == 1), 0.0, 1.0)
        keep_below = jnp.where(last_x & (low == 0), 0.0, 1.0)
        places = (2 * offset - 1) % 8, 2 * offset, 2 * offset + 1, (2 * offset + 2) % 8
        parts = [[], []]
        for u in range(0, units, HD):
            at = pl.ds(u, HD)
            edge = edge_ref[:, at].astype(F32)
            rows = [hidden_ref[place, :, at].astype(F32) for place in places]
            rows[0] = jnp.where(first_x, edge, rows[0]) * keep_above
            rows[3] = jnp.where(last_x, edge, rows[3]) * keep_below
            for r in range(2):
                sums = [
                    taps_ref[pl.ds(b, 1), at] * rows[r]
                    + taps_ref[pl.ds(3 + b, 1), at] * rows[r + 1]
                    + taps_ref[pl.ds(6 + b, 1), at] * rows[r + 2]
                    for b in range(3)
                ]
                conv = (
                    sums[1]
                    + jnp.where(col == 0, 0.0, pltpu.roll(sums[0], 1, 0))
                    + jnp.where(col == cols - 1, 0.0, pltpu.roll(sums[2], cols - 1, 0))
                )
                inner = math.sqrt(2.0 / math.pi) * (conv + 0.044715 * (conv * conv * conv))
                parts[r].append((0.5 * conv * (1.0 + jnp.tanh(inner))).astype(BF16))
        active = jnp.concatenate([jnp.concatenate(p, axis=1) for p in parts], axis=0)
        out = jnp.dot(active, w_ref[...], preferred_element_type=F32)
        top, bottom = out[:cols].astype(BF16), out[cols:].astype(BF16)
        outs[2 * n][...] = jnp.where(core_at == 0, bottom, top)
        outs[2 * n + 1][...] = jnp.where(core_at == 0, top, bottom)


def conv_down(spot, offsets, hidden, edge, taps, weight, hides):
    cols = edge.shape[0]
    shape = jax.ShapeDtypeStruct((cols, weight.shape[1]), BF16)
    args = (spot, hidden, edge, taps, weight)
    return call(
        functools.partial(conv_kernel, offsets),
        "conv_gelu_down",
        14,
        [shape] * (2 * len(offsets)),
        [SMEM] + [VMEM] * (len(args) - 1),
        args,
        hides,
    )


def shift(array, axis, by):
    count = lax.axis_size(axis)
    return lax.ppermute(array, axis, [(i, (i + by) % count) for i in range(count)])


def after_all(array, *others):
    return lax.optimization_barrier((array, *others))[0]


def body(
    stream_in, query_in, key_in, value_in, out_weight, norm_gain, up_weight, conv_taps, down_weight
):
    shape = stream_in.shape
    _, _, cols, dim = shape
    views = lax.axis_size(VIEW)
    near = lax.axis_size(NEAR)
    at = lax.axis_index(NEAR)
    part = up_weight.shape[1] // near
    low = 1 - lax.axis_index("zl")
    spot = jnp.stack(
        [lax.axis_index(name) for name in ("x", "core", "y", "zh")] + [low]
    ).astype(jnp.int32)
    flat = [a.reshape(cols, dim) for a in (stream_in, query_in, key_in, value_in)]

    width = dim // near
    mine = lax.dynamic_slice_in_dim(out_weight, at * width, width, 1)
    mine = lax.all_gather(mine, VIEW, axis=0, tiled=False)

    packed = pack(*flat[1:])
    moved = lax.all_to_all(packed, VIEW, split_axis=0, concat_axis=0, tiled=True)
    attended = attend(moved, cols)
    back = lax.all_to_all(attended, VIEW, split_axis=0, concat_axis=0, tiled=True)

    own_taps = lax.dynamic_slice_in_dim(conv_taps, at * part, part, 2).reshape(-1)
    high = lax.reduce_precision(own_taps, 8, 7)
    middle = lax.reduce_precision(own_taps - high, 8, 7)
    terms = jnp.concatenate([high, middle, own_taps - high - middle])
    terms = jnp.pad(terms, (0, 8 * dim - terms.size)).astype(BF16).reshape(8, dim)
    up_slice = lax.dynamic_slice_in_dim(up_weight, at * part, part, 1).T
    down_slice = lax.dynamic_slice_in_dim(down_weight, at * part, part, 0)
    pair = after_all(jnp.concatenate([up_slice, down_slice, terms]), mine)
    pair = lax.all_gather(pair, VIEW, axis=0, tiled=False)

    half = views // 2
    mine = after_all(mine, moved[0, :8])
    before, after = shift(mine, "x", 1), shift(mine, "x", -1)
    across = jnp.concatenate([shift(before[:half], "x", 1), shift(after[half:], "x", -1)])
    pieces = []
    for piece in (mine, after, across, before):
        pieces += [piece, shift(piece, "core", 1)]
    stream, normed = mix(spot, join(back), flat[0], norm_gain, pieces)

    up_rows = pair[:, :part].reshape(-1, dim)
    down_rows = pair[:, part : 2 * part].reshape(-1, dim)
    taps = pair[:, 2 * part :].reshape(views, -1)[:, : 27 * part].astype(F32)
    taps = jnp.sum(taps.reshape(views, 3, 9, part), axis=1)
    taps = taps.transpose(1, 0, 2).reshape(9, views * part)

    half = cols // 2
    before, after = shift(normed, "x", 1), shift(normed, "x", -1)
    across = jnp.concatenate([shift(before[:half], "x", 1), shift(after[half:], "x", -1)])
    rows = []
    for row in (normed, after, across, before):
        rows += [row, shift(row, "core", 1)]
    hidden, edge = up(spot, rows, up_rows)
    edge = shift(edge, "zl", 1)

    def add(*terms):
        return sum(term.astype(F32) for term in terms).astype(BF16)

    give, keep_2 = conv_down(spot, (2,), hidden, edge, taps, down_rows, False)
    got_2 = shift(give, "core", 1)
    give_1, keep_1, give_3, keep_3, give_0, keep_0 = conv_down(
        spot, (1, 3, 0), hidden, edge, taps, down_rows, True
    )
    got_1, got_3, got_0 = (shift(give, "core", 1) for give in (give_1, give_3, give_0))
    total = add(keep_2, got_2)
    right, left = shift(total[:half], "x", 1), shift(total[half:], "x", -1)
    blank = jnp.zeros_like(left)
    right = add(keep_1, got_1, jnp.concatenate([right, blank]))
    left = add(keep_3, got_3, jnp.concatenate([blank, left]))
    right, left = shift(right, "x", 1), shift(left, "x", -1)
    result = stream
    for term in (keep_0, got_0, right, left):
        result = result + term.astype(F32)
    return result.astype(BF16).reshape(shape)


def solution(mesh):
    fine = Mesh(mesh.devices.reshape(4, 4, 2, 4, 2), ("y", "zh", "zl", "x", "core"))
    tokens = P(VIEW, ROW, None, None)
    return jax.shard_map(
        body,
        mesh=fine,
        in_specs=(
            tokens,
            tokens,
            tokens,
            tokens,
            P(VIEW, None),
            P(),
            P(None, VIEW),
            P(None, None, VIEW),
            P(VIEW, None),
        ),
        out_specs=tokens,
        check_vma=False,
    )
```

```python
import functools
import math

import jax
import jax.numpy as jnp
from jax import lax
from jax.experimental import pallas as pl
from jax.experimental.pallas import tpu as pltpu
from jax.sharding import Mesh, PartitionSpec as P

HD = 128
VIEW = ("y", "zh")
ROW = ("zl", "x", "core")
NEAR = ("x", "core")
F32 = jnp.float32
BF16 = jnp.bfloat16
MIB = 1024 * 1024
VMEM = pl.BlockSpec(memory_space=pltpu.VMEM)
SMEM = pl.BlockSpec(memory_space=pltpu.SMEM)


def call(kernel, name, limit, out_shape, in_specs, args, hides=False, out_specs=None, scratch=()):
    return pl.pallas_call(
        kernel,
        out_shape=out_shape,
        in_specs=in_specs,
        out_specs=out_specs or jax.tree.map(lambda _: VMEM, out_shape),
        scratch_shapes=list(scratch),
        compiler_params=pltpu.CompilerParams(vmem_limit_bytes=limit * MIB),
        cost_estimate=pl.CostEstimate(
            flops=30_000_000_000 if hides else 1000, bytes_accessed=1000, transcendentals=0
        ),
        name=name,
    )(*args)


def pack_kernel(q_ref, k_ref, v_ref, out_ref):
    heads, cols = out_ref.shape[0], q_ref.shape[0]
    for h in range(heads):
        for i, ref in enumerate((q_ref, k_ref, v_ref)):
            out_ref[h, pl.ds(i * cols, cols), :] = ref[:, pl.ds(h * HD, HD)]


def pack(query, key, value):
    cols, dim = query.shape
    shape = jax.ShapeDtypeStruct((dim // HD, 3 * cols, HD), BF16)
    return call(pack_kernel, "pack_heads", 6, shape, [VMEM] * 3, (query, key, value))


def attend_kernel(factor, step, moved_ref, extra_ref, out_ref):
    views, cols = moved_ref.shape[0], moved_ref.shape[1] // 3
    key = moved_ref[:, pl.ds(cols, cols), :].reshape(-1, HD)
    value = moved_ref[:, pl.ds(2 * cols, cols), :].reshape(-1, HD)
    for i in range(0, views, step):
        query = moved_ref[pl.ds(i, step), pl.ds(0, cols), :].reshape(-1, HD)
        scores = lax.dot_general(
            query, key, (((1,), (1,)), ((), ())), preferred_element_type=F32
        )
        top = jnp.max(scores, axis=-1, keepdims=True)
        weights = jnp.exp2((scores - top) * factor)
        total = jnp.sum(weights, axis=-1, keepdims=True)
        mixed = jnp.dot(weights.astype(BF16), value, preferred_element_type=F32) / total
        out_ref[pl.ds(i, step), pl.ds(0, cols), :] = mixed.astype(BF16).reshape(step, cols, HD)
    for i in range(views):
        out_ref[i, pl.ds(cols, extra_ref.shape[0]), :] = extra_ref[...]


def attend(moved, extra, cols):
    factor = math.log2(math.e) / math.sqrt(HD)
    shape = jax.ShapeDtypeStruct((moved.shape[0], cols + extra.shape[0], HD), BF16)
    kernel = functools.partial(attend_kernel, factor, 2)
    return call(kernel, "attend", 24, shape, [VMEM] * 2, (moved, extra), True)


def join_kernel(spot_ref, back_ref, out_ref):
    for j in range(back_ref.shape[0]):
        y, zh = lax.rem(spot_ref[2] + j // 4, 4), lax.rem(spot_ref[3] + j % 4, 4)
        out_ref[:, pl.ds(j * HD, HD)] = back_ref[y * 4 + zh, pl.ds(0, out_ref.shape[0]), :]


def join(spot, back, cols):
    shape = jax.ShapeDtypeStruct((cols, back.shape[0] * HD), BF16)
    return call(join_kernel, "join_heads", 4, shape, [SMEM, VMEM], (spot, back), True)


def mix_kernel(counts, spot_ref, left_ref, stream_ref, gain_ref, *refs):
    w_refs, (stream_out, normed_out, acc, sem) = list(refs[:-4]), refs[-4:]
    width = w_refs[0].shape[2]
    for i, count in enumerate(counts):
        core_at = spot_ref[1] if i % 2 == 0 else 1 - spot_ref[1]
        block = 2 * lax.rem(spot_ref[0] + i // 2, 4) + core_at
        at = pl.ds(pl.multiple_of(block * width, width), width)
        total, first = stream_ref[:, at].astype(F32), 0
        for w_ref in w_refs[:count]:
            weight = w_ref[...].reshape(-1, width)
            left = left_ref[:, pl.ds(first, weight.shape[0])]
            total += jnp.dot(left, weight, preferred_element_type=F32)
            first += weight.shape[0]
        acc[:, at] = total
        w_refs = w_refs[count:]
    copy = pltpu.make_async_copy(acc, stream_out, sem)
    copy.start()
    stream = acc[...]
    scale = lax.rsqrt(jnp.mean(stream * stream, axis=-1, keepdims=True) + 1e-06)
    normed_out[...] = (stream * scale * gain_ref[...]).astype(BF16)
    copy.wait()


def mix(spot, left, stream_in, gain, pieces):
    shapes = [jax.ShapeDtypeStruct(stream_in.shape, t) for t in (F32, BF16)]
    counts = [len(piece) for piece in pieces]
    flat = [array for piece in pieces for array in piece]
    args = (spot, left, stream_in, gain.reshape(1, -1), *flat)
    return call(
        functools.partial(mix_kernel, counts),
        "mix_norm",
        8,
        shapes,
        [SMEM] + [VMEM] * (len(args) - 1),
        args,
        out_specs=[pl.BlockSpec(memory_space=pltpu.HBM), VMEM],
        scratch=[pltpu.VMEM(stream_in.shape, F32), pltpu.SemaphoreType.DMA],
    )


def chip_rows(spot_ref, same, other):
    first = spot_ref[1] == 0
    same = jnp.concatenate([ref[...] for ref in same])
    other = jnp.concatenate([ref[...] for ref in other])
    return [jnp.where(first, same, other), jnp.where(first, other, same)]


def product(rows, w_ref):
    return lax.dot_general(
        jnp.concatenate(rows), w_ref[...], (((1,), (1,)), ((), ())), preferred_element_type=F32
    ).astype(BF16)


def up_most_kernel(spot_ref, *refs):
    rows_refs, (w_ref, out_ref) = refs[:-2], refs[-2:]
    rows = []
    for i in range(0, len(rows_refs), 2):
        rows += chip_rows(spot_ref, rows_refs[i : i + 1], rows_refs[i + 1 : i + 2])
    out_ref[...] = product(rows, w_ref).reshape(out_ref.shape)


def up_most(spot, rows, weight):
    shape = jax.ShapeDtypeStruct((len(rows), rows[0].shape[0], weight.shape[0]), BF16)
    args = (spot, *rows, weight)
    return call(up_most_kernel, "up_most", 14, shape, [SMEM] + [VMEM] * (len(args) - 1), args, True)


def up_last_kernel(spot_ref, *refs):
    rows_refs, (w_ref, most_ref, out_ref, edge_ref) = refs[:-4], refs[-4:]
    half = len(rows_refs) // 2
    rows = chip_rows(spot_ref, rows_refs[:half], rows_refs[half:])
    out_ref[...] = product(rows, w_ref).reshape(out_ref.shape)
    low = spot_ref[4]
    at = 2 * lax.rem(4 - low - spot_ref[0], 4) + low
    edge = most_ref[0]
    for place in range(1, 8):
        ref, index = row_of(most_ref, out_ref, place)
        edge = jnp.where(at == place, ref[index], edge)
    edge_ref[...] = edge


def row_of(most_ref, last_ref, place):
    if place in (4, 5):
        return last_ref, place - 4
    return most_ref, place if place < 4 else place - 2


def up_last(spot, rows, weight, most):
    cols, units = most.shape[1:]
    shapes = [
        jax.ShapeDtypeStruct((2, cols, units), BF16),
        jax.ShapeDtypeStruct((cols, units), BF16),
    ]
    args = (spot, *rows, weight, most)
    return call(up_last_kernel, "up_last", 8, shapes, [SMEM] + [VMEM] * (len(args) - 1), args)


def conv_kernel(offsets, spot_ref, *refs):
    most_ref, last_ref, edge_ref, taps_ref, w_ref, *outs = refs
    cols, units = edge_ref.shape
    core_at, low = spot_ref[1], spot_ref[4]
    col = lax.broadcasted_iota(jnp.int32, (cols, HD), 0)
    for n, offset in enumerate(offsets):
        x_at = lax.rem(spot_ref[0] + offset, 4)
        first_x, last_x = x_at == 0, x_at == 3
        keep_above = jnp.where(first_x & (low == 1), 0.0, 1.0)
        keep_below = jnp.where(last_x & (low == 0), 0.0, 1.0)
        places = [row_of(most_ref, last_ref, (2 * offset + k) % 8) for k in (-1, 0, 1, 2)]
        parts = [[], []]
        for u in range(0, units, HD):
            at = pl.ds(u, HD)
            edge = edge_ref[:, at].astype(F32)
            rows = [ref[index, :, at].astype(F32) for ref, index in places]
            rows[0] = jnp.where(first_x, edge, rows[0]) * keep_above
            rows[3] = jnp.where(last_x, edge, rows[3]) * keep_below
            for r in range(2):
                sums = [
                    taps_ref[pl.ds(b, 1), at] * rows[r]
                    + taps_ref[pl.ds(3 + b, 1), at] * rows[r + 1]
                    + taps_ref[pl.ds(6 + b, 1), at] * rows[r + 2]
                    for b in range(3)
                ]
                conv = (
                    sums[1]
                    + jnp.where(col == 0, 0.0, pltpu.roll(sums[0], 1, 0))
                    + jnp.where(col == cols - 1, 0.0, pltpu.roll(sums[2], cols - 1, 0))
                )
                inner = math.sqrt(2.0 / math.pi) * (conv + 0.044715 * (conv * conv * conv))
                parts[r].append((0.5 * conv * (1.0 + jnp.tanh(inner))).astype(BF16))
        active = jnp.concatenate([jnp.concatenate(p, axis=1) for p in parts], axis=0)
        out = jnp.dot(active, w_ref[...], preferred_element_type=F32)
        top, bottom = out[:cols].astype(BF16), out[cols:].astype(BF16)
        outs[2 * n][...] = jnp.where(core_at == 0, bottom, top)
        outs[2 * n + 1][...] = jnp.where(core_at == 0, top, bottom)


def conv_down(spot, offsets, most, last, edge, taps, weight, hides):
    cols = edge.shape[0]
    shape = jax.ShapeDtypeStruct((cols, weight.shape[1]), BF16)
    args = (spot, most, last, edge, taps, weight)
    return call(
        functools.partial(conv_kernel, offsets),
        "conv_gelu_down",
        14,
        [shape] * (2 * len(offsets)),
        [SMEM] + [VMEM] * (len(args) - 1),
        args,
        hides,
    )


def shift(array, axis, by):
    count = lax.axis_size(axis)
    return lax.ppermute(array, axis, [(i, (i + by) % count) for i in range(count)])


def after_all(array, *others):
    return lax.optimization_barrier((array, *others))[0]


def gather4(array, axis):
    return [array, shift(array, axis, -1), shift(array, axis, 2), shift(array, axis, 1)]


def body(
    stream_in, query_in, key_in, value_in, out_weight, norm_gain, up_weight, conv_taps, down_weight
):
    shape = stream_in.shape
    _, _, cols, dim = shape
    views = lax.axis_size(VIEW)
    near = lax.axis_size(NEAR)
    at = lax.axis_index(NEAR)
    part = up_weight.shape[1] // near
    low = 1 - lax.axis_index("zl")
    spot = jnp.stack(
        [lax.axis_index(name) for name in ("x", "core", "y", "zh")] + [low]
    ).astype(jnp.int32)
    flat = [a.reshape(cols, dim) for a in (stream_in, query_in, key_in, value_in)]

    width = dim // near
    mine = lax.dynamic_slice_in_dim(out_weight, at * width, width, 1)
    mine = jnp.stack(gather4(mine, "zh"))

    packed, mine = lax.optimization_barrier((pack(*flat[1:]), mine))
    moved = lax.all_to_all(packed, VIEW, split_axis=0, concat_axis=0, tiled=True)

    own_taps = lax.dynamic_slice_in_dim(conv_taps, at * part, part, 2).reshape(-1)
    high = lax.reduce_precision(own_taps, 8, 7)
    middle = lax.reduce_precision(own_taps - high, 8, 7)
    terms = jnp.concatenate([high, middle, own_taps - high - middle])
    term_rows = 16 * pl.cdiv(terms.size, 16 * HD)
    terms = jnp.pad(terms, (0, term_rows * HD - terms.size)).astype(BF16).reshape(term_rows, HD)
    attended = attend(moved, terms, cols)
    back = lax.all_to_all(attended, VIEW, split_axis=0, concat_axis=0, tiled=True)

    half = views // 2
    mine = jnp.concatenate(gather4(mine, "y"))
    before, after = shift(mine, "x", 1), shift(mine, "x", -1)
    across = [shift(before[:half], "x", 1), shift(after[half:], "x", -1)]
    pieces = []
    for piece in ([mine], [after], across, [before]):
        pieces += [piece, [shift(array, "core", 1) for array in piece]]

    up_slice = lax.dynamic_slice_in_dim(up_weight, at * part, part, 1).T
    down_slice = lax.dynamic_slice_in_dim(down_weight, at * part, part, 0)
    pair = after_all(jnp.concatenate([up_slice, down_slice]), mine)
    pair = lax.all_gather(pair, VIEW, axis=0, tiled=False)
    up_rows = pair[:, :part].reshape(-1, dim)
    down_rows = pair[:, part:].reshape(-1, dim)

    stream, normed = mix(spot, join(spot, back, cols), flat[0], norm_gain, pieces)
    taps = back[:, cols:].reshape(views, -1)[:, : 27 * part].astype(F32)
    taps = jnp.sum(taps.reshape(views, 3, 9, part), axis=1)
    taps = taps.transpose(1, 0, 2).reshape(9, views * part)

    half = cols // 2
    before, after = shift(normed, "x", 1), shift(normed, "x", -1)
    across = [shift(before[:half], "x", 1), shift(after[half:], "x", -1)]
    rows = []
    for row in (normed, after, before):
        rows += [row, shift(row, "core", 1)]
    most = up_most(spot, rows, up_rows)
    across = [after_all(array, taps) for array in across]
    across += [shift(array, "core", 1) for array in across]
    last, edge = up_last(spot, across, up_rows, most)
    edge = shift(edge, "zl", 1)

    def add(*terms):
        return sum(term.astype(F32) for term in terms).astype(BF16)

    give, keep_2 = conv_down(spot, (2,), most, last, edge, taps, down_rows, False)
    got_2 = shift(give, "core", 1)
    give_1, keep_1, give_3, keep_3, give_0, keep_0 = conv_down(
        spot, (1, 3, 0), most, last, edge, taps, down_rows, True
    )
    got_1, got_3, got_0 = (shift(give, "core", 1) for give in (give_1, give_3, give_0))
    total = add(keep_2, got_2)
    right, left = shift(total[:half], "x", 1), shift(total[half:], "x", -1)
    blank = jnp.zeros_like(left)
    right = add(keep_1, got_1, jnp.concatenate([right, blank]))
    left = add(keep_3, got_3, jnp.concatenate([blank, left]))
    right, left = shift(right, "x", 1), shift(left, "x", -1)
    result = stream
    for term in (keep_0, got_0, right, left):
        result = result + term.astype(F32)
    return result.astype(BF16).reshape(shape)


def solution(mesh):
    fine = Mesh(mesh.devices.reshape(4, 4, 2, 4, 2), ("y", "zh", "zl", "x", "core"))
    tokens = P(VIEW, ROW, None, None)
    return jax.shard_map(
        body,
        mesh=fine,
        in_specs=(
            tokens,
            tokens,
            tokens,
            tokens,
            P(VIEW, None),
            P(),
            P(None, VIEW),
            P(None, None, VIEW),
            P(VIEW, None),
        ),
        out_specs=tokens,
        check_vma=False,
    )
```

```python
import functools
import math

import jax
import jax.numpy as jnp
from jax import lax
from jax.experimental import pallas as pl
from jax.experimental.pallas import tpu as pltpu
from jax.sharding import Mesh, PartitionSpec as P

HD = 128
VIEW = ("y", "zh")
ROW = ("zl", "x", "core")
NEAR = ("x", "core")
F32 = jnp.float32
BF16 = jnp.bfloat16
MIB = 1024 * 1024
VMEM = pl.BlockSpec(memory_space=pltpu.VMEM)
SMEM = pl.BlockSpec(memory_space=pltpu.SMEM)


def call(kernel, name, limit, out_shape, in_specs, args, hides=False, out_specs=None, scratch=()):
    return pl.pallas_call(
        kernel,
        out_shape=out_shape,
        in_specs=in_specs,
        out_specs=out_specs or jax.tree.map(lambda _: VMEM, out_shape),
        scratch_shapes=list(scratch),
        compiler_params=pltpu.CompilerParams(vmem_limit_bytes=limit * MIB),
        cost_estimate=pl.CostEstimate(
            flops=30_000_000_000 if hides else 1000, bytes_accessed=1000, transcendentals=0
        ),
        name=name,
    )(*args)


def pack_kernel(q_ref, k_ref, v_ref, out_ref, held, sems):
    heads, cols = out_ref.shape[0], q_ref.shape[0]
    copies = [
        pltpu.make_async_copy(ref, held.at[i], sems.at[i])
        for i, ref in enumerate((q_ref, k_ref, v_ref))
    ]
    for copy in copies:
        copy.start()
    for i, copy in enumerate(copies):
        copy.wait()
        for h in range(heads):
            out_ref[h, pl.ds(i * cols, cols), :] = held[i, :, pl.ds(h * HD, HD)]


def pack(query, key, value):
    cols, dim = query.shape
    shape = jax.ShapeDtypeStruct((dim // HD, 3 * cols, HD), BF16)
    return call(
        pack_kernel,
        "pack_heads",
        58,
        shape,
        [pl.BlockSpec(memory_space=pltpu.HBM)] * 3,
        (query, key, value),
        scratch=[pltpu.VMEM((3, cols, dim), BF16), pltpu.SemaphoreType.DMA((3,))],
    )


def attend_kernel(factor, step, moved_ref, extra_ref, out_ref):
    views, cols = moved_ref.shape[0], moved_ref.shape[1] // 3
    key = moved_ref[:, pl.ds(cols, cols), :].reshape(-1, HD)
    value = moved_ref[:, pl.ds(2 * cols, cols), :].reshape(-1, HD)
    for i in range(0, views, step):
        query = moved_ref[pl.ds(i, step), pl.ds(0, cols), :].reshape(-1, HD)
        scores = lax.dot_general(
            query, key, (((1,), (1,)), ((), ())), preferred_element_type=F32
        )
        top = jnp.max(scores, axis=-1, keepdims=True)
        weights = jnp.exp2((scores - top) * factor)
        total = jnp.sum(weights, axis=-1, keepdims=True)
        mixed = jnp.dot(weights.astype(BF16), value, preferred_element_type=F32) / total
        out_ref[pl.ds(i, step), pl.ds(0, cols), :] = mixed.astype(BF16).reshape(step, cols, HD)
    for i in range(views):
        out_ref[i, pl.ds(cols, extra_ref.shape[0]), :] = extra_ref[...]


def attend(moved, extra, cols):
    factor = math.log2(math.e) / math.sqrt(HD)
    shape = jax.ShapeDtypeStruct((moved.shape[0], cols + extra.shape[0], HD), BF16)
    kernel = functools.partial(attend_kernel, factor, 2)
    return call(kernel, "attend", 24, shape, [VMEM] * 2, (moved, extra), True)


def join_kernel(spot_ref, back_ref, out_ref):
    for j in range(back_ref.shape[0]):
        y, zh = lax.rem(spot_ref[2] + j // 4, 4), lax.rem(spot_ref[3] + j % 4, 4)
        out_ref[:, pl.ds(j * HD, HD)] = back_ref[y * 4 + zh, pl.ds(0, out_ref.shape[0]), :]


def join(spot, back, cols):
    shape = jax.ShapeDtypeStruct((cols, back.shape[0] * HD), BF16)
    return call(join_kernel, "join_heads", 4, shape, [SMEM, VMEM], (spot, back), True)


def mix_kernel(counts, spot_ref, left_ref, stream_ref, gain_ref, *refs):
    w_refs, (stream_out, normed_out, acc, sem) = list(refs[:-4]), refs[-4:]
    width = w_refs[0].shape[2]
    for i, count in enumerate(counts):
        core_at = spot_ref[1] if i % 2 == 0 else 1 - spot_ref[1]
        block = 2 * lax.rem(spot_ref[0] + i // 2, 4) + core_at
        at = pl.ds(pl.multiple_of(block * width, width), width)
        total, first = stream_ref[:, at].astype(F32), 0
        for w_ref in w_refs[:count]:
            weight = w_ref[...].reshape(-1, width)
            left = left_ref[:, pl.ds(first, weight.shape[0])]
            total += jnp.dot(left, weight, preferred_element_type=F32)
            first += weight.shape[0]
        acc[:, at] = total
        w_refs = w_refs[count:]
    copy = pltpu.make_async_copy(acc, stream_out, sem)
    copy.start()
    stream = acc[...]
    scale = lax.rsqrt(jnp.mean(stream * stream, axis=-1, keepdims=True) + 1e-06)
    normed_out[...] = (stream * scale * gain_ref[...]).astype(BF16)
    copy.wait()


def mix(spot, left, stream_in, gain, pieces):
    shapes = [jax.ShapeDtypeStruct(stream_in.shape, t) for t in (F32, BF16)]
    counts = [len(piece) for piece in pieces]
    flat = [array for piece in pieces for array in piece]
    args = (spot, left, stream_in, gain.reshape(1, -1), *flat)
    return call(
        functools.partial(mix_kernel, counts),
        "mix_norm",
        8,
        shapes,
        [SMEM] + [VMEM] * (len(args) - 1),
        args,
        out_specs=[pl.BlockSpec(memory_space=pltpu.HBM), VMEM],
        scratch=[pltpu.VMEM(stream_in.shape, F32), pltpu.SemaphoreType.DMA],
    )


def chip_rows(spot_ref, same, other):
    first = spot_ref[1] == 0
    same = jnp.concatenate([ref[...] for ref in same])
    other = jnp.concatenate([ref[...] for ref in other])
    return [jnp.where(first, same, other), jnp.where(first, other, same)]


def product(rows, w_ref):
    return lax.dot_general(
        jnp.concatenate(rows), w_ref[...], (((1,), (1,)), ((), ())), preferred_element_type=F32
    ).astype(BF16)


def up_most_kernel(spot_ref, *refs):
    rows_refs, (w_ref, out_ref) = refs[:-2], refs[-2:]
    rows = []
    for i in range(0, len(rows_refs), 2):
        rows += chip_rows(spot_ref, rows_refs[i : i + 1], rows_refs[i + 1 : i + 2])
    out_ref[...] = product(rows, w_ref).reshape(out_ref.shape)


def up_most(spot, rows, weight):
    shape = jax.ShapeDtypeStruct((len(rows), rows[0].shape[0], weight.shape[0]), BF16)
    args = (spot, *rows, weight)
    return call(up_most_kernel, "up_most", 14, shape, [SMEM] + [VMEM] * (len(args) - 1), args, True)


def up_last_kernel(spot_ref, *refs):
    rows_refs, (w_ref, most_ref, out_ref, edge_ref) = refs[:-4], refs[-4:]
    half = len(rows_refs) // 2
    rows = chip_rows(spot_ref, rows_refs[:half], rows_refs[half:])
    out_ref[...] = product(rows, w_ref).reshape(out_ref.shape)
    low = spot_ref[4]
    at = 2 * lax.rem(4 - low - spot_ref[0], 4) + low
    edge = most_ref[0]
    for place in range(1, 8):
        ref, index = row_of(most_ref, out_ref, place)
        edge = jnp.where(at == place, ref[index], edge)
    edge_ref[...] = edge


def row_of(most_ref, last_ref, place):
    if place in (4, 5):
        return last_ref, place - 4
    return most_ref, place if place < 4 else place - 2


def up_last(spot, rows, weight, most):
    cols, units = most.shape[1:]
    shapes = [
        jax.ShapeDtypeStruct((2, cols, units), BF16),
        jax.ShapeDtypeStruct((cols, units), BF16),
    ]
    args = (spot, *rows, weight, most)
    return call(up_last_kernel, "up_last", 8, shapes, [SMEM] + [VMEM] * (len(args) - 1), args)


def conv_kernel(offsets, spot_ref, *refs):
    most_ref, last_ref, edge_ref, taps_ref, w_ref, *outs = refs
    cols, units = edge_ref.shape
    core_at, low = spot_ref[1], spot_ref[4]
    col = lax.broadcasted_iota(jnp.int32, (cols, HD), 0)
    for n, offset in enumerate(offsets):
        x_at = lax.rem(spot_ref[0] + offset, 4)
        first_x, last_x = x_at == 0, x_at == 3
        keep_above = jnp.where(first_x & (low == 1), 0.0, 1.0)
        keep_below = jnp.where(last_x & (low == 0), 0.0, 1.0)
        places = [row_of(most_ref, last_ref, (2 * offset + k) % 8) for k in (-1, 0, 1, 2)]
        parts = [[], []]
        for u in range(0, units, HD):
            at = pl.ds(u, HD)
            edge = edge_ref[:, at].astype(F32)
            rows = [ref[index, :, at].astype(F32) for ref, index in places]
            rows[0] = jnp.where(first_x, edge, rows[0]) * keep_above
            rows[3] = jnp.where(last_x, edge, rows[3]) * keep_below
            for r in range(2):
                sums = [
                    taps_ref[pl.ds(b, 1), at] * rows[r]
                    + taps_ref[pl.ds(3 + b, 1), at] * rows[r + 1]
                    + taps_ref[pl.ds(6 + b, 1), at] * rows[r + 2]
                    for b in range(3)
                ]
                conv = (
                    sums[1]
                    + jnp.where(col == 0, 0.0, pltpu.roll(sums[0], 1, 0))
                    + jnp.where(col == cols - 1, 0.0, pltpu.roll(sums[2], cols - 1, 0))
                )
                inner = math.sqrt(2.0 / math.pi) * (conv + 0.044715 * (conv * conv * conv))
                parts[r].append((0.5 * conv * (1.0 + jnp.tanh(inner))).astype(BF16))
        active = jnp.concatenate([jnp.concatenate(p, axis=1) for p in parts], axis=0)
        out = jnp.dot(active, w_ref[...], preferred_element_type=F32)
        top, bottom = out[:cols].astype(BF16), out[cols:].astype(BF16)
        outs[2 * n][...] = jnp.where(core_at == 0, bottom, top)
        outs[2 * n + 1][...] = jnp.where(core_at == 0, top, bottom)


def conv_down(spot, offsets, most, last, edge, taps, weight, hides):
    cols = edge.shape[0]
    shape = jax.ShapeDtypeStruct((cols, weight.shape[1]), BF16)
    args = (spot, most, last, edge, taps, weight)
    return call(
        functools.partial(conv_kernel, offsets),
        "conv_gelu_down",
        14,
        [shape] * (2 * len(offsets)),
        [SMEM] + [VMEM] * (len(args) - 1),
        args,
        hides,
    )


def shift(array, axis, by):
    count = lax.axis_size(axis)
    return lax.ppermute(array, axis, [(i, (i + by) % count) for i in range(count)])


def after_all(array, *others):
    return lax.optimization_barrier((array, *others))[0]


def gather4(array, axis):
    return [array, shift(array, axis, -1), shift(array, axis, 2), shift(array, axis, 1)]


def body(
    stream_in, query_in, key_in, value_in, out_weight, norm_gain, up_weight, conv_taps, down_weight
):
    shape = stream_in.shape
    _, _, cols, dim = shape
    views = lax.axis_size(VIEW)
    near = lax.axis_size(NEAR)
    at = lax.axis_index(NEAR)
    part = up_weight.shape[1] // near
    low = 1 - lax.axis_index("zl")
    spot = jnp.stack(
        [lax.axis_index(name) for name in ("x", "core", "y", "zh")] + [low]
    ).astype(jnp.int32)
    flat = [a.reshape(cols, dim) for a in (stream_in, query_in, key_in, value_in)]

    width = dim // near
    mine = lax.dynamic_slice_in_dim(out_weight, at * width, width, 1)
    mine = jnp.stack(gather4(mine, "zh"))

    packed, strips = lax.optimization_barrier((pack(*flat[1:]), mine))
    moved = lax.all_to_all(packed, VIEW, split_axis=0, concat_axis=0, tiled=True)

    own_taps = lax.dynamic_slice_in_dim(conv_taps, at * part, part, 2).reshape(-1)
    high = lax.reduce_precision(own_taps, 8, 7)
    middle = lax.reduce_precision(own_taps - high, 8, 7)
    terms = jnp.concatenate([high, middle, own_taps - high - middle])
    term_rows = 16 * pl.cdiv(terms.size, 16 * HD)
    terms = jnp.pad(terms, (0, term_rows * HD - terms.size)).astype(BF16).reshape(term_rows, HD)
    attended = attend(moved, terms, cols)
    back = lax.all_to_all(attended, VIEW, split_axis=0, concat_axis=0, tiled=True)

    half = views // 2
    mine = jnp.concatenate(gather4(strips, "y"))
    before, after = shift(mine, "x", 1), shift(mine, "x", -1)
    across = [shift(before[:half], "x", 1), shift(after[half:], "x", -1)]
    pieces = []
    for piece in ([mine], [after], across, [before]):
        pieces += [piece, [shift(array, "core", 1) for array in piece]]

    up_slice = lax.dynamic_slice_in_dim(up_weight, at * part, part, 1).T
    down_slice = lax.dynamic_slice_in_dim(down_weight, at * part, part, 0)
    pair = after_all(jnp.concatenate([up_slice, down_slice]), strips)
    pair = lax.all_gather(pair, VIEW, axis=0, tiled=False)
    up_rows = pair[:, :part].reshape(-1, dim)
    down_rows = pair[:, part:].reshape(-1, dim)

    stream, normed = mix(spot, join(spot, back, cols), flat[0], norm_gain, pieces)
    taps = back[:, cols:].reshape(views, -1)[:, : 27 * part].astype(F32)
    taps = jnp.sum(taps.reshape(views, 3, 9, part), axis=1)
    taps = taps.transpose(1, 0, 2).reshape(9, views * part)

    half = cols // 2
    before, after = shift(normed, "x", 1), shift(normed, "x", -1)
    across = [shift(before[:half], "x", 1), shift(after[half:], "x", -1)]
    rows = []
    for row in (normed, after, before):
        rows += [row, shift(row, "core", 1)]
    most = up_most(spot, rows, up_rows)
    across = [after_all(array, taps, most) for array in across]
    across += [shift(array, "core", 1) for array in across]
    last, edge = up_last(spot, across, up_rows, most)
    edge = shift(edge, "zl", 1)

    def add(*terms):
        return sum(term.astype(F32) for term in terms).astype(BF16)

    give, keep_2 = conv_down(spot, (2,), most, last, edge, taps, down_rows, False)
    got_2 = shift(give, "core", 1)
    give_1, keep_1, give_3, keep_3, give_0, keep_0 = conv_down(
        spot, (1, 3, 0), most, last, edge, taps, down_rows, True
    )
    got_1, got_3, got_0 = (shift(give, "core", 1) for give in (give_1, give_3, give_0))
    total = add(keep_2, got_2)
    right, left = shift(total[:half], "x", 1), shift(total[half:], "x", -1)
    blank = jnp.zeros_like(left)
    right = add(keep_1, got_1, jnp.concatenate([right, blank]))
    left = add(keep_3, got_3, jnp.concatenate([blank, left]))
    right, left = shift(right, "x", 1), shift(left, "x", -1)
    result = stream
    for term in (keep_0, got_0, right, left):
        result = result + term.astype(F32)
    return result.astype(BF16).reshape(shape)


def solution(mesh):
    fine = Mesh(mesh.devices.reshape(4, 4, 2, 4, 2), ("y", "zh", "zl", "x", "core"))
    tokens = P(VIEW, ROW, None, None)
    return jax.shard_map(
        body,
        mesh=fine,
        in_specs=(
            tokens,
            tokens,
            tokens,
            tokens,
            P(VIEW, None),
            P(),
            P(None, VIEW),
            P(None, None, VIEW),
            P(VIEW, None),
        ),
        out_specs=tokens,
        check_vma=False,
    )
```

```python
import functools
import math

import jax
import jax.numpy as jnp
from jax import lax
from jax.experimental import pallas as pl
from jax.experimental.pallas import tpu as pltpu
from jax.sharding import Mesh, PartitionSpec as P

HD = 128
VIEW = ("y", "zh")
ROW = ("zl", "x", "core")
NEAR = ("x", "core")
F32 = jnp.float32
BF16 = jnp.bfloat16
MIB = 1024 * 1024
VMEM = pl.BlockSpec(memory_space=pltpu.VMEM)
SMEM = pl.BlockSpec(memory_space=pltpu.SMEM)


def call(kernel, name, limit, out_shape, in_specs, args, hides=False, out_specs=None, scratch=()):
    return pl.pallas_call(
        kernel,
        out_shape=out_shape,
        in_specs=in_specs,
        out_specs=out_specs or jax.tree.map(lambda _: VMEM, out_shape),
        scratch_shapes=list(scratch),
        compiler_params=pltpu.CompilerParams(vmem_limit_bytes=limit * MIB),
        cost_estimate=pl.CostEstimate(
            flops=30_000_000_000 if hides else 1000, bytes_accessed=1000, transcendentals=0
        ),
        name=name,
    )(*args)


def pack_kernel(q_ref, k_ref, v_ref, out_ref, held, sems):
    heads, cols = out_ref.shape[0], q_ref.shape[0]
    copies = [
        pltpu.make_async_copy(ref, held.at[i], sems.at[i])
        for i, ref in enumerate((q_ref, k_ref, v_ref))
    ]
    for copy in copies:
        copy.start()
    for i, copy in enumerate(copies):
        copy.wait()
        for h in range(heads):
            out_ref[h, pl.ds(i * cols, cols), :] = held[i, :, pl.ds(h * HD, HD)]


def pack(query, key, value):
    cols, dim = query.shape
    shape = jax.ShapeDtypeStruct((dim // HD, 3 * cols, HD), BF16)
    return call(
        pack_kernel,
        "pack_heads",
        58,
        shape,
        [pl.BlockSpec(memory_space=pltpu.HBM)] * 3,
        (query, key, value),
        scratch=[pltpu.VMEM((3, cols, dim), BF16), pltpu.SemaphoreType.DMA((3,))],
    )


def attend_kernel(factor, step, moved_ref, extra_ref, out_ref):
    views, cols = moved_ref.shape[0], moved_ref.shape[1] // 3
    key = moved_ref[:, pl.ds(cols, cols), :].reshape(-1, HD)
    value = moved_ref[:, pl.ds(2 * cols, cols), :].reshape(-1, HD)
    for i in range(0, views, step):
        query = moved_ref[pl.ds(i, step), pl.ds(0, cols), :].reshape(-1, HD)
        scores = lax.dot_general(
            query, key, (((1,), (1,)), ((), ())), preferred_element_type=F32
        )
        top = jnp.max(scores, axis=-1, keepdims=True)
        weights = jnp.exp2((scores - top) * factor)
        total = jnp.sum(weights, axis=-1, keepdims=True)
        mixed = jnp.dot(weights.astype(BF16), value, preferred_element_type=F32) / total
        out_ref[pl.ds(i, step), pl.ds(0, cols), :] = mixed.astype(BF16).reshape(step, cols, HD)
    for i in range(views):
        out_ref[i, pl.ds(cols, extra_ref.shape[0]), :] = extra_ref[...]


def attend(moved, extra, cols):
    factor = math.log2(math.e) / math.sqrt(HD)
    shape = jax.ShapeDtypeStruct((moved.shape[0], cols + extra.shape[0], HD), BF16)
    kernel = functools.partial(attend_kernel, factor, 2)
    return call(kernel, "attend", 24, shape, [VMEM] * 2, (moved, extra), True)


def join_kernel(spot_ref, back_ref, out_ref):
    for j in range(back_ref.shape[0]):
        y, zh = lax.rem(spot_ref[2] + j // 4, 4), lax.rem(spot_ref[3] + j % 4, 4)
        out_ref[:, pl.ds(j * HD, HD)] = back_ref[y * 4 + zh, pl.ds(0, out_ref.shape[0]), :]


def join(spot, back, cols):
    shape = jax.ShapeDtypeStruct((cols, back.shape[0] * HD), BF16)
    return call(join_kernel, "join_heads", 4, shape, [SMEM, VMEM], (spot, back), True)


def mix_kernel(counts, spot_ref, left_ref, stream_ref, gain_ref, *refs):
    w_refs, (stream_out, normed_out, acc, sem) = list(refs[:-4]), refs[-4:]
    width = w_refs[0].shape[2]
    for i, count in enumerate(counts):
        core_at = spot_ref[1] if i % 2 == 0 else 1 - spot_ref[1]
        block = 2 * lax.rem(spot_ref[0] + i // 2, 4) + core_at
        at = pl.ds(pl.multiple_of(block * width, width), width)
        total, first = stream_ref[:, at].astype(F32), 0
        for w_ref in w_refs[:count]:
            weight = w_ref[...].reshape(-1, width)
            left = left_ref[:, pl.ds(first, weight.shape[0])]
            total += jnp.dot(left, weight, preferred_element_type=F32)
            first += weight.shape[0]
        acc[:, at] = total
        w_refs = w_refs[count:]
    copy = pltpu.make_async_copy(acc, stream_out, sem)
    copy.start()
    stream = acc[...]
    scale = lax.rsqrt(jnp.mean(stream * stream, axis=-1, keepdims=True) + 1e-06)
    normed_out[...] = (stream * scale * gain_ref[...]).astype(BF16)
    copy.wait()


def mix(spot, left, stream_in, gain, pieces):
    shapes = [jax.ShapeDtypeStruct(stream_in.shape, t) for t in (F32, BF16)]
    counts = [len(piece) for piece in pieces]
    flat = [array for piece in pieces for array in piece]
    args = (spot, left, stream_in, gain.reshape(1, -1), *flat)
    return call(
        functools.partial(mix_kernel, counts),
        "mix_norm",
        14,
        shapes,
        [SMEM] + [VMEM] * (len(args) - 1),
        args,
        out_specs=[pl.BlockSpec(memory_space=pltpu.HBM), VMEM],
        scratch=[pltpu.VMEM(stream_in.shape, F32), pltpu.SemaphoreType.DMA],
    )


def chip_rows(spot_ref, same, other):
    first = spot_ref[1] == 0
    same = jnp.concatenate([ref[...] for ref in same])
    other = jnp.concatenate([ref[...] for ref in other])
    return [jnp.where(first, same, other), jnp.where(first, other, same)]


def product(rows, w_ref):
    return lax.dot_general(
        jnp.concatenate(rows), w_ref[...], (((1,), (1,)), ((), ())), preferred_element_type=F32
    ).astype(BF16)


def up_most_kernel(spot_ref, *refs):
    rows_refs, (w_ref, out_ref) = refs[:-2], refs[-2:]
    rows = []
    for i in range(0, len(rows_refs), 2):
        rows += chip_rows(spot_ref, rows_refs[i : i + 1], rows_refs[i + 1 : i + 2])
    out_ref[...] = product(rows, w_ref).reshape(out_ref.shape)


def up_most(spot, rows, weight):
    shape = jax.ShapeDtypeStruct((len(rows), rows[0].shape[0], weight.shape[0]), BF16)
    args = (spot, *rows, weight)
    return call(up_most_kernel, "up_most", 14, shape, [SMEM] + [VMEM] * (len(args) - 1), args, True)


def up_last_kernel(spot_ref, *refs):
    rows_refs, (w_ref, most_ref, out_ref, edge_ref) = refs[:-4], refs[-4:]
    half = len(rows_refs) // 2
    rows = chip_rows(spot_ref, rows_refs[:half], rows_refs[half:])
    out_ref[...] = product(rows, w_ref).reshape(out_ref.shape)
    low = spot_ref[4]
    at = 2 * lax.rem(4 - low - spot_ref[0], 4) + low
    edge = most_ref[0]
    for place in range(1, 8):
        ref, index = row_of(most_ref, out_ref, place)
        edge = jnp.where(at == place, ref[index], edge)
    edge_ref[...] = edge


def row_of(most_ref, last_ref, place):
    if place in (4, 5):
        return last_ref, place - 4
    return most_ref, place if place < 4 else place - 2


def up_last(spot, rows, weight, most):
    cols, units = most.shape[1:]
    shapes = [
        jax.ShapeDtypeStruct((2, cols, units), BF16),
        jax.ShapeDtypeStruct((cols, units), BF16),
    ]
    args = (spot, *rows, weight, most)
    return call(up_last_kernel, "up_last", 8, shapes, [SMEM] + [VMEM] * (len(args) - 1), args)


def conv_kernel(offsets, spot_ref, *refs):
    most_ref, last_ref, edge_ref, taps_ref, w_ref, *outs = refs
    cols, units = edge_ref.shape
    core_at, low = spot_ref[1], spot_ref[4]
    col = lax.broadcasted_iota(jnp.int32, (cols, HD), 0)
    for n, offset in enumerate(offsets):
        x_at = lax.rem(spot_ref[0] + offset, 4)
        first_x, last_x = x_at == 0, x_at == 3
        keep_above = jnp.where(first_x & (low == 1), 0.0, 1.0)
        keep_below = jnp.where(last_x & (low == 0), 0.0, 1.0)
        places = [row_of(most_ref, last_ref, (2 * offset + k) % 8) for k in (-1, 0, 1, 2)]
        parts = [[], []]
        for u in range(0, units, HD):
            at = pl.ds(u, HD)
            edge = edge_ref[:, at].astype(F32)
            rows = [ref[index, :, at].astype(F32) for ref, index in places]
            rows[0] = jnp.where(first_x, edge, rows[0]) * keep_above
            rows[3] = jnp.where(last_x, edge, rows[3]) * keep_below
            for r in range(2):
                sums = [
                    taps_ref[pl.ds(b, 1), at] * rows[r]
                    + taps_ref[pl.ds(3 + b, 1), at] * rows[r + 1]
                    + taps_ref[pl.ds(6 + b, 1), at] * rows[r + 2]
                    for b in range(3)
                ]
                conv = (
                    sums[1]
                    + jnp.where(col == 0, 0.0, pltpu.roll(sums[0], 1, 0))
                    + jnp.where(col == cols - 1, 0.0, pltpu.roll(sums[2], cols - 1, 0))
                )
                inner = math.sqrt(2.0 / math.pi) * (conv + 0.044715 * (conv * conv * conv))
                parts[r].append((0.5 * conv * (1.0 + jnp.tanh(inner))).astype(BF16))
        active = jnp.concatenate([jnp.concatenate(p, axis=1) for p in parts], axis=0)
        out = jnp.dot(active, w_ref[...], preferred_element_type=F32)
        top, bottom = out[:cols].astype(BF16), out[cols:].astype(BF16)
        outs[2 * n][...] = jnp.where(core_at == 0, bottom, top)
        outs[2 * n + 1][...] = jnp.where(core_at == 0, top, bottom)


def conv_down(spot, offsets, most, last, edge, taps, weight, hides):
    cols = edge.shape[0]
    shape = jax.ShapeDtypeStruct((cols, weight.shape[1]), BF16)
    args = (spot, most, last, edge, taps, weight)
    return call(
        functools.partial(conv_kernel, offsets),
        "conv_gelu_down",
        14,
        [shape] * (2 * len(offsets)),
        [SMEM] + [VMEM] * (len(args) - 1),
        args,
        hides,
    )


def shift(array, axis, by):
    count = lax.axis_size(axis)
    return lax.ppermute(array, axis, [(i, (i + by) % count) for i in range(count)])


def after_all(array, *others):
    return lax.optimization_barrier((array, *others))[0]


def gather4(array, axis):
    return [array, shift(array, axis, -1), shift(array, axis, 2), shift(array, axis, 1)]


def ring(array, axis):
    half = array.shape[0] // 2
    before, after = shift(array, axis, 1), shift(array, axis, -1)
    across = shift(before[:half], axis, 1), shift(after[half:], axis, -1)
    return jnp.concatenate([array, after, *across, before])


def body(
    stream_in, query_in, key_in, value_in, out_weight, norm_gain, up_weight, conv_taps, down_weight
):
    shape = stream_in.shape
    _, _, cols, dim = shape
    views = lax.axis_size(VIEW)
    near = lax.axis_size(NEAR)
    at = lax.axis_index(NEAR)
    part = up_weight.shape[1] // near
    low = 1 - lax.axis_index("zl")
    spot = jnp.stack(
        [lax.axis_index(name) for name in ("x", "core", "y", "zh")] + [low]
    ).astype(jnp.int32)
    flat = [a.reshape(cols, dim) for a in (stream_in, query_in, key_in, value_in)]

    width = dim // near
    mine = lax.dynamic_slice_in_dim(out_weight, at * width, width, 1)
    mine = jnp.stack(gather4(mine, "zh"))

    packed, strips = lax.optimization_barrier((pack(*flat[1:]), mine))
    moved = lax.all_to_all(packed, VIEW, split_axis=0, concat_axis=0, tiled=True)

    own_taps = lax.dynamic_slice_in_dim(conv_taps, at * part, part, 2).reshape(-1)
    high = lax.reduce_precision(own_taps, 8, 7)
    middle = lax.reduce_precision(own_taps - high, 8, 7)
    terms = jnp.concatenate([high, middle, own_taps - high - middle])
    term_rows = 16 * pl.cdiv(terms.size, 16 * HD)
    terms = jnp.pad(terms, (0, term_rows * HD - terms.size)).astype(BF16).reshape(term_rows, HD)
    attended = attend(moved, terms, cols)
    back = lax.all_to_all(attended, VIEW, split_axis=0, concat_axis=0, tiled=True)

    half = views // 2
    mine = jnp.concatenate(gather4(strips, "y"))
    before, after = shift(mine, "x", 1), shift(mine, "x", -1)
    mine, before, after, seen = lax.optimization_barrier((mine, before, after, attended))
    later = seen[0, 0, 0] * 0
    across = [shift(before[:half] + later, "x", 1), shift(after[half:] + later, "x", -1)]
    pieces = []
    for piece in ([mine], [after], across, [before]):
        pieces += [piece, [shift(array, "core", 1) for array in piece]]

    up_slice = lax.dynamic_slice_in_dim(up_weight, at * part, part, 1).T
    down_slice = lax.dynamic_slice_in_dim(down_weight, at * part, part, 0)
    pair = jnp.stack([up_slice, down_slice]) + moved[0, 0, 0] * 0
    before, after = shift(pair, "zh", 1), shift(pair, "zh", -1)
    across = shift(before[0], "zh", 1), shift(after[1], "zh", -1)
    up_part, down_part = (
        jnp.concatenate([pair[i], after[i], across[i], before[i]]) for i in range(2)
    )
    up_rows = ring(up_part, "y")
    down_rows = ring(after_all(down_part, up_rows), "y")

    stream, normed = mix(spot, join(spot, back, cols), flat[0], norm_gain, pieces)
    taps = back[:, cols:].reshape(views, -1)[:, : 27 * part].astype(F32)
    taps = jnp.sum(taps.reshape(4, 4, 3, 9, part), axis=2)
    for axis, name in enumerate(("y", "zh")):
        taps = lax.dynamic_slice_in_dim(
            jnp.concatenate([taps, taps], axis=axis), lax.axis_index(name), 4, axis
        )
    taps = taps.transpose(2, 0, 1, 3).reshape(9, views * part)

    half = cols // 2
    before, after = shift(normed, "x", 1), shift(normed, "x", -1)
    across = [shift(before[:half], "x", 1), shift(after[half:], "x", -1)]
    rows = []
    for row in (normed, after, before):
        rows += [row, shift(row, "core", 1)]
    most = up_most(spot, rows, up_rows)
    across = [after_all(array, taps, most) for array in across]
    across += [shift(array, "core", 1) for array in across]
    last, edge = up_last(spot, across, up_rows, most)
    edge = shift(edge, "zl", 1)

    def add(*terms):
        return sum(term.astype(F32) for term in terms).astype(BF16)

    give, keep_2 = conv_down(spot, (2,), most, last, edge, taps, down_rows, False)
    got_2 = shift(give, "core", 1)
    give_1, keep_1, give_3, keep_3, give_0, keep_0 = conv_down(
        spot, (1, 3, 0), most, last, edge, taps, down_rows, True
    )
    got_1, got_3, got_0 = (shift(give, "core", 1) for give in (give_1, give_3, give_0))
    total = add(keep_2, got_2)
    right, left = shift(total[:half], "x", 1), shift(total[half:], "x", -1)
    blank = jnp.zeros_like(left)
    right = add(keep_1, got_1, jnp.concatenate([right, blank]))
    left = add(keep_3, got_3, jnp.concatenate([blank, left]))
    right, left = shift(right, "x", 1), shift(left, "x", -1)
    result = stream
    for term in (keep_0, got_0, right, left):
        result = result + term.astype(F32)
    return result.astype(BF16).reshape(shape)


def solution(mesh):
    fine = Mesh(mesh.devices.reshape(4, 4, 2, 4, 2), ("y", "zh", "zl", "x", "core"))
    tokens = P(VIEW, ROW, None, None)
    return jax.shard_map(
        body,
        mesh=fine,
        in_specs=(
            tokens,
            tokens,
            tokens,
            tokens,
            P(VIEW, None),
            P(),
            P(None, VIEW),
            P(None, None, VIEW),
            P(VIEW, None),
        ),
        out_specs=tokens,
        check_vma=False,
    )
```

```python
import functools
import math

import jax
import jax.numpy as jnp
from jax import lax
from jax.experimental import pallas as pl
from jax.experimental.pallas import tpu as pltpu
from jax.sharding import Mesh, PartitionSpec as P

HD = 128
VIEW = ("y", "zh")
ROW = ("zl", "x", "core")
NEAR = ("x", "core")
F32 = jnp.float32
BF16 = jnp.bfloat16
MIB = 1024 * 1024
VMEM = pl.BlockSpec(memory_space=pltpu.VMEM)
SMEM = pl.BlockSpec(memory_space=pltpu.SMEM)


def call(kernel, name, limit, out_shape, in_specs, args, hides=False, out_specs=None, scratch=()):
    return pl.pallas_call(
        kernel,
        out_shape=out_shape,
        in_specs=in_specs,
        out_specs=out_specs or jax.tree.map(lambda _: VMEM, out_shape),
        scratch_shapes=list(scratch),
        compiler_params=pltpu.CompilerParams(vmem_limit_bytes=limit * MIB),
        cost_estimate=pl.CostEstimate(
            flops=30_000_000_000 if hides else 1000, bytes_accessed=1000, transcendentals=0
        ),
        name=name,
    )(*args)


def pack_kernel(q_ref, k_ref, v_ref, out_ref, held, sems):
    heads, cols = out_ref.shape[0], q_ref.shape[0]
    copies = [
        pltpu.make_async_copy(ref, held.at[i], sems.at[i])
        for i, ref in enumerate((q_ref, k_ref, v_ref))
    ]
    for copy in copies:
        copy.start()
    for i, copy in enumerate(copies):
        copy.wait()
        for h in range(heads):
            out_ref[h, pl.ds(i * cols, cols), :] = held[i, :, pl.ds(h * HD, HD)]


def pack(query, key, value):
    cols, dim = query.shape
    shape = jax.ShapeDtypeStruct((dim // HD, 3 * cols, HD), BF16)
    return call(
        pack_kernel,
        "pack_heads",
        58,
        shape,
        [pl.BlockSpec(memory_space=pltpu.HBM)] * 3,
        (query, key, value),
        scratch=[pltpu.VMEM((3, cols, dim), BF16), pltpu.SemaphoreType.DMA((3,))],
    )


def attend_kernel(factor, step, moved_ref, extra_ref, out_ref):
    views, cols = moved_ref.shape[0], moved_ref.shape[1] // 3
    key = moved_ref[:, pl.ds(cols, cols), :].reshape(-1, HD)
    value = moved_ref[:, pl.ds(2 * cols, cols), :].reshape(-1, HD)
    for i in range(0, views, step):
        query = moved_ref[pl.ds(i, step), pl.ds(0, cols), :].reshape(-1, HD)
        scores = lax.dot_general(
            query, key, (((1,), (1,)), ((), ())), preferred_element_type=F32
        )
        top = jnp.max(scores, axis=-1, keepdims=True)
        weights = jnp.exp2((scores - top) * factor)
        total = jnp.sum(weights, axis=-1, keepdims=True)
        mixed = jnp.dot(weights.astype(BF16), value, preferred_element_type=F32) / total
        out_ref[pl.ds(i, step), pl.ds(0, cols), :] = mixed.astype(BF16).reshape(step, cols, HD)
    for i in range(views):
        out_ref[i, pl.ds(cols, extra_ref.shape[0]), :] = extra_ref[...]


def attend(moved, extra, cols):
    factor = math.log2(math.e) / math.sqrt(HD)
    shape = jax.ShapeDtypeStruct((moved.shape[0], cols + extra.shape[0], HD), BF16)
    kernel = functools.partial(attend_kernel, factor, 2)
    return call(kernel, "attend", 24, shape, [VMEM] * 2, (moved, extra), True)


def join_kernel(spot_ref, back_ref, out_ref):
    for j in range(back_ref.shape[0]):
        y, zh = lax.rem(spot_ref[2] + j // 4, 4), lax.rem(spot_ref[3] + j % 4, 4)
        out_ref[:, pl.ds(j * HD, HD)] = back_ref[y * 4 + zh, pl.ds(0, out_ref.shape[0]), :]


def join(spot, back, cols):
    shape = jax.ShapeDtypeStruct((cols, back.shape[0] * HD), BF16)
    return call(join_kernel, "join_heads", 4, shape, [SMEM, VMEM], (spot, back), True)


def mix_kernel(counts, spot_ref, left_ref, stream_ref, gain_ref, *refs):
    w_refs, (stream_out, normed_out, acc, sem) = list(refs[:-4]), refs[-4:]
    width = w_refs[0].shape[2]
    for i, count in enumerate(counts):
        core_at = spot_ref[1] if i % 2 == 0 else 1 - spot_ref[1]
        block = 2 * lax.rem(spot_ref[0] + i // 2, 4) + core_at
        at = pl.ds(pl.multiple_of(block * width, width), width)
        total, first = stream_ref[:, at].astype(F32), 0
        for w_ref in w_refs[:count]:
            weight = w_ref[...].reshape(-1, width)
            left = left_ref[:, pl.ds(first, weight.shape[0])]
            total += jnp.dot(left, weight, preferred_element_type=F32)
            first += weight.shape[0]
        acc[:, at] = total
        w_refs = w_refs[count:]
    copy = pltpu.make_async_copy(acc, stream_out, sem)
    copy.start()
    stream = acc[...]
    scale = lax.rsqrt(jnp.mean(stream * stream, axis=-1, keepdims=True) + 1e-06)
    normed_out[...] = (stream * scale * gain_ref[...]).astype(BF16)
    copy.wait()


def mix(spot, left, stream_in, gain, pieces):
    shapes = [jax.ShapeDtypeStruct(stream_in.shape, t) for t in (F32, BF16)]
    counts = [len(piece) for piece in pieces]
    flat = [array for piece in pieces for array in piece]
    args = (spot, left, stream_in, gain.reshape(1, -1), *flat)
    return call(
        functools.partial(mix_kernel, counts),
        "mix_norm",
        8,
        shapes,
        [SMEM] + [VMEM] * (len(args) - 1),
        args,
        out_specs=[pl.BlockSpec(memory_space=pltpu.HBM), VMEM],
        scratch=[pltpu.VMEM(stream_in.shape, F32), pltpu.SemaphoreType.DMA],
    )


def chip_rows(spot_ref, same, other):
    first = spot_ref[1] == 0
    same = jnp.concatenate([ref[...] for ref in same])
    other = jnp.concatenate([ref[...] for ref in other])
    return [jnp.where(first, same, other), jnp.where(first, other, same)]


def product(rows, w_ref):
    return lax.dot_general(
        jnp.concatenate(rows), w_ref[...], (((1,), (1,)), ((), ())), preferred_element_type=F32
    ).astype(BF16)


def up_most_kernel(spot_ref, *refs):
    rows_refs, (w_ref, out_ref) = refs[:-2], refs[-2:]
    rows = []
    for i in range(0, len(rows_refs), 2):
        rows += chip_rows(spot_ref, rows_refs[i : i + 1], rows_refs[i + 1 : i + 2])
    out_ref[...] = product(rows, w_ref).reshape(out_ref.shape)


def up_most(spot, rows, weight):
    shape = jax.ShapeDtypeStruct((len(rows), rows[0].shape[0], weight.shape[0]), BF16)
    args = (spot, *rows, weight)
    return call(up_most_kernel, "up_most", 14, shape, [SMEM] + [VMEM] * (len(args) - 1), args, True)


def up_last_kernel(spot_ref, *refs):
    rows_refs, (w_ref, most_ref, out_ref, edge_ref) = refs[:-4], refs[-4:]
    half = len(rows_refs) // 2
    rows = chip_rows(spot_ref, rows_refs[:half], rows_refs[half:])
    out_ref[...] = product(rows, w_ref).reshape(out_ref.shape)
    low = spot_ref[4]
    at = 2 * lax.rem(4 - low - spot_ref[0], 4) + low
    edge = most_ref[0]
    for place in range(1, 8):
        ref, index = row_of(most_ref, out_ref, place)
        edge = jnp.where(at == place, ref[index], edge)
    edge_ref[...] = edge


def row_of(most_ref, last_ref, place):
    if place in (4, 5):
        return last_ref, place - 4
    return most_ref, place if place < 4 else place - 2


def up_last(spot, rows, weight, most):
    cols, units = most.shape[1:]
    shapes = [
        jax.ShapeDtypeStruct((2, cols, units), BF16),
        jax.ShapeDtypeStruct((cols, units), BF16),
    ]
    args = (spot, *rows, weight, most)
    return call(up_last_kernel, "up_last", 8, shapes, [SMEM] + [VMEM] * (len(args) - 1), args)


def conv_kernel(offsets, spot_ref, *refs):
    most_ref, last_ref, edge_ref, taps_ref, w_ref, *outs = refs
    cols, units = edge_ref.shape
    core_at, low = spot_ref[1], spot_ref[4]
    col = lax.broadcasted_iota(jnp.int32, (cols, HD), 0)
    for n, offset in enumerate(offsets):
        x_at = lax.rem(spot_ref[0] + offset, 4)
        first_x, last_x = x_at == 0, x_at == 3
        keep_above = jnp.where(first_x & (low == 1), 0.0, 1.0)
        keep_below = jnp.where(last_x & (low == 0), 0.0, 1.0)
        places = [row_of(most_ref, last_ref, (2 * offset + k) % 8) for k in (-1, 0, 1, 2)]
        parts = [[], []]
        for u in range(0, units, HD):
            at = pl.ds(u, HD)
            edge = edge_ref[:, at].astype(F32)
            rows = [ref[index, :, at].astype(F32) for ref, index in places]
            rows[0] = jnp.where(first_x, edge, rows[0]) * keep_above
            rows[3] = jnp.where(last_x, edge, rows[3]) * keep_below
            for r in range(2):
                sums = [
                    taps_ref[pl.ds(b, 1), at] * rows[r]
                    + taps_ref[pl.ds(3 + b, 1), at] * rows[r + 1]
                    + taps_ref[pl.ds(6 + b, 1), at] * rows[r + 2]
                    for b in range(3)
                ]
                conv = (
                    sums[1]
                    + jnp.where(col == 0, 0.0, pltpu.roll(sums[0], 1, 0))
                    + jnp.where(col == cols - 1, 0.0, pltpu.roll(sums[2], cols - 1, 0))
                )
                inner = math.sqrt(2.0 / math.pi) * (conv + 0.044715 * (conv * conv * conv))
                parts[r].append((0.5 * conv * (1.0 + jnp.tanh(inner))).astype(BF16))
        active = jnp.concatenate([jnp.concatenate(p, axis=1) for p in parts], axis=0)
        out = jnp.dot(active, w_ref[...], preferred_element_type=F32)
        top, bottom = out[:cols].astype(BF16), out[cols:].astype(BF16)
        outs[2 * n][...] = jnp.where(core_at == 0, bottom, top)
        outs[2 * n + 1][...] = jnp.where(core_at == 0, top, bottom)


def conv_down(spot, offsets, most, last, edge, taps, weight, hides):
    cols = edge.shape[0]
    shape = jax.ShapeDtypeStruct((cols, weight.shape[1]), BF16)
    args = (spot, most, last, edge, taps, weight)
    return call(
        functools.partial(conv_kernel, offsets),
        "conv_gelu_down",
        14,
        [shape] * (2 * len(offsets)),
        [SMEM] + [VMEM] * (len(args) - 1),
        args,
        hides,
    )


def shift(array, axis, by):
    count = lax.axis_size(axis)
    return lax.ppermute(array, axis, [(i, (i + by) % count) for i in range(count)])


def after_all(array, *others):
    return lax.optimization_barrier((array, *others))[0]


def gather4(array, axis):
    return [array, shift(array, axis, -1), shift(array, axis, 2), shift(array, axis, 1)]


def body(
    stream_in, query_in, key_in, value_in, out_weight, norm_gain, up_weight, conv_taps, down_weight
):
    shape = stream_in.shape
    _, _, cols, dim = shape
    views = lax.axis_size(VIEW)
    near = lax.axis_size(NEAR)
    at = lax.axis_index(NEAR)
    part = up_weight.shape[1] // near
    low = 1 - lax.axis_index("zl")
    spot = jnp.stack(
        [lax.axis_index(name) for name in ("x", "core", "y", "zh")] + [low]
    ).astype(jnp.int32)
    flat = [a.reshape(cols, dim) for a in (stream_in, query_in, key_in, value_in)]

    width = dim // near
    mine = lax.dynamic_slice_in_dim(out_weight, at * width, width, 1)
    mine = jnp.stack(gather4(mine, "zh"))

    packed, strips = lax.optimization_barrier((pack(*flat[1:]), mine))
    moved = lax.all_to_all(packed, VIEW, split_axis=0, concat_axis=0, tiled=True)

    own_taps = lax.dynamic_slice_in_dim(conv_taps, at * part, part, 2).reshape(-1)
    high = lax.reduce_precision(own_taps, 8, 7)
    middle = lax.reduce_precision(own_taps - high, 8, 7)
    terms = jnp.concatenate([high, middle, own_taps - high - middle])
    term_rows = 16 * pl.cdiv(terms.size, 16 * HD)
    terms = jnp.pad(terms, (0, term_rows * HD - terms.size)).astype(BF16).reshape(term_rows, HD)
    attended = attend(moved, terms, cols)
    back = lax.all_to_all(attended, VIEW, split_axis=0, concat_axis=0, tiled=True)

    half = views // 2
    mine = jnp.concatenate(gather4(strips, "y"))
    before, after = shift(mine, "x", 1), shift(mine, "x", -1)
    across = [shift(before[:half], "x", 1), shift(after[half:], "x", -1)]
    pieces = []
    for piece in ([mine], [after], across, [before]):
        pieces += [piece, [shift(array, "core", 1) for array in piece]]

    up_slice = lax.dynamic_slice_in_dim(up_weight, at * part, part, 1).T
    down_slice = lax.dynamic_slice_in_dim(down_weight, at * part, part, 0)
    pair = after_all(jnp.concatenate([up_slice, down_slice]), mine)
    pair = lax.all_gather(pair, VIEW, axis=0, tiled=False)
    up_rows = pair[:, :part].reshape(-1, dim)

    stream, normed = mix(spot, join(spot, back, cols), flat[0], norm_gain, pieces)
    taps = back[:, cols:].reshape(views, -1)[:, : 27 * part].astype(F32)
    taps = jnp.sum(taps.reshape(views, 3, 9, part), axis=1)
    taps = taps.transpose(1, 0, 2).reshape(9, views * part)

    half = cols // 2
    before, after = shift(normed, "x", 1), shift(normed, "x", -1)
    across = [shift(before[:half], "x", 1), shift(after[half:], "x", -1)]
    rows = []
    for row in (normed, after, before):
        rows += [row, shift(row, "core", 1)]
    most = up_most(spot, rows, up_rows)
    across = [after_all(array, taps, most) for array in across]
    across += [shift(array, "core", 1) for array in across]
    last, edge_sent = up_last(spot, across, up_rows, most)
    edge = shift(edge_sent, "zl", 1)
    down_rows = after_all(pair, edge_sent)[:, part:].reshape(-1, dim)

    def add(*terms):
        return sum(term.astype(F32) for term in terms).astype(BF16)

    give, keep_2 = conv_down(spot, (2,), most, last, edge, taps, down_rows, False)
    got_2 = shift(give, "core", 1)
    give_1, keep_1, give_3, keep_3, give_0, keep_0 = conv_down(
        spot, (1, 3, 0), most, last, edge, taps, down_rows, True
    )
    got_1, got_3, got_0 = (shift(give, "core", 1) for give in (give_1, give_3, give_0))
    total = add(keep_2, got_2)
    right, left = shift(total[:half], "x", 1), shift(total[half:], "x", -1)
    blank = jnp.zeros_like(left)
    right = add(keep_1, got_1, jnp.concatenate([right, blank]))
    left = add(keep_3, got_3, jnp.concatenate([blank, left]))
    right, left = shift(right, "x", 1), shift(left, "x", -1)
    result = stream
    for term in (keep_0, got_0, right, left):
        result = result + term.astype(F32)
    return result.astype(BF16).reshape(shape)


def solution(mesh):
    fine = Mesh(mesh.devices.reshape(4, 4, 2, 4, 2), ("y", "zh", "zl", "x", "core"))
    tokens = P(VIEW, ROW, None, None)
    return jax.shard_map(
        body,
        mesh=fine,
        in_specs=(
            tokens,
            tokens,
            tokens,
            tokens,
            P(VIEW, None),
            P(),
            P(None, VIEW),
            P(None, None, VIEW),
            P(VIEW, None),
        ),
        out_specs=tokens,
        check_vma=False,
    )
```

```python
import functools
import math

import jax
import jax.numpy as jnp
from jax import lax
from jax.experimental import pallas as pl
from jax.experimental.pallas import tpu as pltpu
from jax.sharding import Mesh, PartitionSpec as P

HD = 128
VIEW = ("y", "zh")
ROW = ("zl", "x", "core")
NEAR = ("x", "core")
F32 = jnp.float32
BF16 = jnp.bfloat16
MIB = 1024 * 1024
VMEM = pl.BlockSpec(memory_space=pltpu.VMEM)
SMEM = pl.BlockSpec(memory_space=pltpu.SMEM)


def call(kernel, name, limit, out_shape, in_specs, args, hides=False, out_specs=None, scratch=()):
    return pl.pallas_call(
        kernel,
        out_shape=out_shape,
        in_specs=in_specs,
        out_specs=out_specs or jax.tree.map(lambda _: VMEM, out_shape),
        scratch_shapes=list(scratch),
        compiler_params=pltpu.CompilerParams(vmem_limit_bytes=limit * MIB),
        cost_estimate=pl.CostEstimate(
            flops=15_000_000_000 if hides else 1000, bytes_accessed=1000, transcendentals=0
        ),
        name=name,
    )(*args)


def pack_kernel(q_ref, k_ref, v_ref, out_ref, held, sems):
    heads, cols = out_ref.shape[0], q_ref.shape[0]
    copies = [
        pltpu.make_async_copy(ref, held.at[i], sems.at[i])
        for i, ref in enumerate((q_ref, k_ref, v_ref))
    ]
    for copy in copies:
        copy.start()
    for i, copy in enumerate(copies):
        copy.wait()
        for h in range(heads):
            out_ref[h, pl.ds(i * cols, cols), :] = held[i, :, pl.ds(h * HD, HD)]


def pack(query, key, value):
    cols, dim = query.shape
    shape = jax.ShapeDtypeStruct((dim // HD, 3 * cols, HD), BF16)
    return call(
        pack_kernel,
        "pack_heads",
        58,
        shape,
        [pl.BlockSpec(memory_space=pltpu.HBM)] * 3,
        (query, key, value),
        scratch=[pltpu.VMEM((3, cols, dim), BF16), pltpu.SemaphoreType.DMA((3,))],
    )


def attend_kernel(factor, step, moved_ref, extra_ref, out_ref):
    views, cols = moved_ref.shape[0], moved_ref.shape[1] // 3
    key = moved_ref[:, pl.ds(cols, cols), :].reshape(-1, HD)
    value = moved_ref[:, pl.ds(2 * cols, cols), :].reshape(-1, HD)
    for i in range(0, views, step):
        query = moved_ref[pl.ds(i, step), pl.ds(0, cols), :].reshape(-1, HD)
        scores = lax.dot_general(
            query, key, (((1,), (1,)), ((), ())), preferred_element_type=F32
        )
        top = jnp.max(scores, axis=-1, keepdims=True)
        weights = jnp.exp2((scores - top) * factor)
        total = jnp.sum(weights, axis=-1, keepdims=True)
        mixed = jnp.dot(weights.astype(BF16), value, preferred_element_type=F32) / total
        out_ref[pl.ds(i, step), pl.ds(0, cols), :] = mixed.astype(BF16).reshape(step, cols, HD)
    for i in range(views):
        out_ref[i, pl.ds(cols, extra_ref.shape[0]), :] = extra_ref[...]


def attend(moved, extra, cols):
    factor = math.log2(math.e) / math.sqrt(HD)
    shape = jax.ShapeDtypeStruct((moved.shape[0], cols + extra.shape[0], HD), BF16)
    kernel = functools.partial(attend_kernel, factor, 2)
    return call(kernel, "attend", 24, shape, [VMEM] * 2, (moved, extra), True)


def join_kernel(spot_ref, back_ref, out_ref):
    for j in range(back_ref.shape[0]):
        y, zh = lax.rem(spot_ref[2] + j // 4, 4), lax.rem(spot_ref[3] + j % 4, 4)
        out_ref[:, pl.ds(j * HD, HD)] = back_ref[y * 4 + zh, pl.ds(0, out_ref.shape[0]), :]


def join(spot, back, cols):
    shape = jax.ShapeDtypeStruct((cols, back.shape[0] * HD), BF16)
    return call(join_kernel, "join_heads", 4, shape, [SMEM, VMEM], (spot, back), True)


def mix_kernel(counts, spot_ref, left_ref, stream_ref, gain_ref, *refs):
    w_refs, (stream_out, normed_out, acc, sem) = list(refs[:-4]), refs[-4:]
    width = w_refs[0].shape[2]
    for i, count in enumerate(counts):
        core_at = spot_ref[1] if i % 2 == 0 else 1 - spot_ref[1]
        block = 2 * lax.rem(spot_ref[0] + i // 2, 4) + core_at
        at = pl.ds(pl.multiple_of(block * width, width), width)
        total, first = stream_ref[:, at].astype(F32), 0
        for w_ref in w_refs[:count]:
            weight = w_ref[...].reshape(-1, width)
            left = left_ref[:, pl.ds(first, weight.shape[0])]
            total += jnp.dot(left, weight, preferred_element_type=F32)
            first += weight.shape[0]
        acc[:, at] = total
        w_refs = w_refs[count:]
    copy = pltpu.make_async_copy(acc, stream_out, sem)
    copy.start()
    stream = acc[...]
    scale = lax.rsqrt(jnp.mean(stream * stream, axis=-1, keepdims=True) + 1e-06)
    normed_out[...] = (stream * scale * gain_ref[...]).astype(BF16)
    copy.wait()


def mix(spot, left, stream_in, gain, pieces):
    shapes = [jax.ShapeDtypeStruct(stream_in.shape, t) for t in (F32, BF16)]
    counts = [len(piece) for piece in pieces]
    flat = [array for piece in pieces for array in piece]
    args = (spot, left, stream_in, gain.reshape(1, -1), *flat)
    return call(
        functools.partial(mix_kernel, counts),
        "mix_norm",
        8,
        shapes,
        [SMEM] + [VMEM] * (len(args) - 1),
        args,
        out_specs=[pl.BlockSpec(memory_space=pltpu.HBM), VMEM],
        scratch=[pltpu.VMEM(stream_in.shape, F32), pltpu.SemaphoreType.DMA],
    )


def chip_rows(spot_ref, same, other):
    first = spot_ref[1] == 0
    same = jnp.concatenate([ref[...] for ref in same])
    other = jnp.concatenate([ref[...] for ref in other])
    return [jnp.where(first, same, other), jnp.where(first, other, same)]


def product(rows, w_ref):
    return lax.dot_general(
        jnp.concatenate(rows), w_ref[...], (((1,), (1,)), ((), ())), preferred_element_type=F32
    ).astype(BF16)


def up_most_kernel(spot_ref, *refs):
    rows_refs, (w_ref, out_ref) = refs[:-2], refs[-2:]
    rows = []
    for i in range(0, len(rows_refs), 2):
        rows += chip_rows(spot_ref, rows_refs[i : i + 1], rows_refs[i + 1 : i + 2])
    out_ref[...] = product(rows, w_ref).reshape(out_ref.shape)


def up_most(spot, rows, weight):
    shape = jax.ShapeDtypeStruct((len(rows), rows[0].shape[0], weight.shape[0]), BF16)
    args = (spot, *rows, weight)
    return call(up_most_kernel, "up_most", 14, shape, [SMEM] + [VMEM] * (len(args) - 1), args, True)


def up_last_kernel(spot_ref, *refs):
    rows_refs, (w_ref, most_ref, out_ref, edge_ref) = refs[:-4], refs[-4:]
    half = len(rows_refs) // 2
    rows = chip_rows(spot_ref, rows_refs[:half], rows_refs[half:])
    out_ref[...] = product(rows, w_ref).reshape(out_ref.shape)
    low = spot_ref[4]
    at = 2 * lax.rem(4 - low - spot_ref[0], 4) + low
    edge = most_ref[0]
    for place in range(1, 8):
        ref, index = row_of(most_ref, out_ref, place)
        edge = jnp.where(at == place, ref[index], edge)
    edge_ref[...] = edge


def row_of(most_ref, last_ref, place):
    if place in (4, 5):
        return last_ref, place - 4
    return most_ref, place if place < 4 else place - 2


def up_last(spot, rows, weight, most):
    cols, units = most.shape[1:]
    shapes = [
        jax.ShapeDtypeStruct((2, cols, units), BF16),
        jax.ShapeDtypeStruct((cols, units), BF16),
    ]
    args = (spot, *rows, weight, most)
    return call(up_last_kernel, "up_last", 8, shapes, [SMEM] + [VMEM] * (len(args) - 1), args)


def conv_kernel(offsets, spot_ref, *refs):
    most_ref, last_ref, edge_ref, taps_ref, w_ref, *outs = refs
    cols, units = edge_ref.shape
    core_at, low = spot_ref[1], spot_ref[4]
    col = lax.broadcasted_iota(jnp.int32, (cols, HD), 0)
    for n, offset in enumerate(offsets):
        x_at = lax.rem(spot_ref[0] + offset, 4)
        first_x, last_x = x_at == 0, x_at == 3
        keep_above = jnp.where(first_x & (low == 1), 0.0, 1.0)
        keep_below = jnp.where(last_x & (low == 0), 0.0, 1.0)
        places = [row_of(most_ref, last_ref, (2 * offset + k) % 8) for k in (-1, 0, 1, 2)]
        parts = [[], []]
        for u in range(0, units, HD):
            at = pl.ds(u, HD)
            edge = edge_ref[:, at].astype(F32)
            rows = [ref[index, :, at].astype(F32) for ref, index in places]
            rows[0] = jnp.where(first_x, edge, rows[0]) * keep_above
            rows[3] = jnp.where(last_x, edge, rows[3]) * keep_below
            for r in range(2):
                sums = [
                    taps_ref[pl.ds(b, 1), at] * rows[r]
                    + taps_ref[pl.ds(3 + b, 1), at] * rows[r + 1]
                    + taps_ref[pl.ds(6 + b, 1), at] * rows[r + 2]
                    for b in range(3)
                ]
                conv = (
                    sums[1]
                    + jnp.where(col == 0, 0.0, pltpu.roll(sums[0], 1, 0))
                    + jnp.where(col == cols - 1, 0.0, pltpu.roll(sums[2], cols - 1, 0))
                )
                inner = math.sqrt(2.0 / math.pi) * (conv + 0.044715 * (conv * conv * conv))
                parts[r].append((0.5 * conv * (1.0 + jnp.tanh(inner))).astype(BF16))
        active = jnp.concatenate([jnp.concatenate(p, axis=1) for p in parts], axis=0)
        out = jnp.dot(active, w_ref[...], preferred_element_type=F32)
        top, bottom = out[:cols].astype(BF16), out[cols:].astype(BF16)
        outs[2 * n][...] = jnp.where(core_at == 0, bottom, top)
        outs[2 * n + 1][...] = jnp.where(core_at == 0, top, bottom)


def conv_down(spot, offsets, most, last, edge, taps, weight, hides):
    cols = edge.shape[0]
    shape = jax.ShapeDtypeStruct((cols, weight.shape[1]), BF16)
    args = (spot, most, last, edge, taps, weight)
    return call(
        functools.partial(conv_kernel, offsets),
        "conv_gelu_down",
        14,
        [shape] * (2 * len(offsets)),
        [SMEM] + [VMEM] * (len(args) - 1),
        args,
        hides,
    )


def shift(array, axis, by):
    count = lax.axis_size(axis)
    return lax.ppermute(array, axis, [(i, (i + by) % count) for i in range(count)])


def after_all(array, *others):
    return lax.optimization_barrier((array, *others))[0]


def gather4(array, axis):
    return [array, shift(array, axis, -1), shift(array, axis, 2), shift(array, axis, 1)]


def body(
    stream_in, query_in, key_in, value_in, out_weight, norm_gain, up_weight, conv_taps, down_weight
):
    shape = stream_in.shape
    _, _, cols, dim = shape
    views = lax.axis_size(VIEW)
    near = lax.axis_size(NEAR)
    at = lax.axis_index(NEAR)
    part = up_weight.shape[1] // near
    low = 1 - lax.axis_index("zl")
    spot = jnp.stack(
        [lax.axis_index(name) for name in ("x", "core", "y", "zh")] + [low]
    ).astype(jnp.int32)
    flat = [a.reshape(cols, dim) for a in (stream_in, query_in, key_in, value_in)]

    width = dim // near
    mine = lax.dynamic_slice_in_dim(out_weight, at * width, width, 1)
    mine = jnp.stack(gather4(mine, "zh"))

    packed, strips = lax.optimization_barrier((pack(*flat[1:]), mine))
    moved = lax.all_to_all(packed, VIEW, split_axis=0, concat_axis=0, tiled=True)

    own_taps = lax.dynamic_slice_in_dim(conv_taps, at * part, part, 2).reshape(-1)
    high = lax.reduce_precision(own_taps, 8, 7)
    middle = lax.reduce_precision(own_taps - high, 8, 7)
    terms = jnp.concatenate([high, middle, own_taps - high - middle])
    term_rows = 16 * pl.cdiv(terms.size, 16 * HD)
    terms = jnp.pad(terms, (0, term_rows * HD - terms.size)).astype(BF16).reshape(term_rows, HD)
    attended = attend(moved, terms, cols)
    back = lax.all_to_all(attended, VIEW, split_axis=0, concat_axis=0, tiled=True)

    half = views // 2
    mine = jnp.concatenate(gather4(strips, "y"))
    before, after = shift(mine, "x", 1), shift(mine, "x", -1)
    across = [shift(before[:half], "x", 1), shift(after[half:], "x", -1)]
    pieces = []
    for piece in ([mine], [after], across, [before]):
        pieces += [piece, [shift(array, "core", 1) for array in piece]]

    up_slice = lax.dynamic_slice_in_dim(up_weight, at * part, part, 1).T
    down_slice = lax.dynamic_slice_in_dim(down_weight, at * part, part, 0)
    up_slice, down_slice = after_all(up_slice, strips), after_all(down_slice, mine)
    up_rows = lax.all_gather(up_slice, VIEW, axis=0, tiled=True)
    down_rows = lax.all_gather(down_slice, VIEW, axis=0, tiled=True)

    stream, normed = mix(spot, join(spot, back, cols), flat[0], norm_gain, pieces)
    taps = back[:, cols:].reshape(views, -1)[:, : 27 * part].astype(F32)
    taps = jnp.sum(taps.reshape(views, 3, 9, part), axis=1)
    taps = taps.transpose(1, 0, 2).reshape(9, views * part)

    half = cols // 2
    before, after = shift(normed, "x", 1), shift(normed, "x", -1)
    across = [shift(before[:half], "x", 1), shift(after[half:], "x", -1)]
    rows = []
    for row in (normed, after, before):
        rows += [row, shift(row, "core", 1)]
    most = up_most(spot, rows, up_rows)
    across = [after_all(array, taps, most) for array in across]
    across += [shift(array, "core", 1) for array in across]
    last, edge = up_last(spot, across, up_rows, most)
    edge = shift(edge, "zl", 1)

    def add(*terms):
        return sum(term.astype(F32) for term in terms).astype(BF16)

    give, keep_2 = conv_down(spot, (2,), most, last, edge, taps, down_rows, False)
    got_2 = shift(give, "core", 1)
    give_1, keep_1, give_3, keep_3, give_0, keep_0 = conv_down(
        spot, (1, 3, 0), most, last, edge, taps, down_rows, True
    )
    got_1, got_3, got_0 = (shift(give, "core", 1) for give in (give_1, give_3, give_0))
    total = add(keep_2, got_2)
    right, left = shift(total[:half], "x", 1), shift(total[half:], "x", -1)
    blank = jnp.zeros_like(left)
    right = add(keep_1, got_1, jnp.concatenate([right, blank]))
    left = add(keep_3, got_3, jnp.concatenate([blank, left]))
    right, left = shift(right, "x", 1), shift(left, "x", -1)
    result = stream
    for term in (keep_0, got_0, right, left):
        result = result + term.astype(F32)
    return result.astype(BF16).reshape(shape)


def solution(mesh):
    fine = Mesh(mesh.devices.reshape(4, 4, 2, 4, 2), ("y", "zh", "zl", "x", "core"))
    tokens = P(VIEW, ROW, None, None)
    return jax.shard_map(
        body,
        mesh=fine,
        in_specs=(
            tokens,
            tokens,
            tokens,
            tokens,
            P(VIEW, None),
            P(),
            P(None, VIEW),
            P(None, None, VIEW),
            P(VIEW, None),
        ),
        out_specs=tokens,
        check_vma=False,
    )
```

```python
import functools
import math

import jax
import jax.numpy as jnp
from jax import lax
from jax.experimental import pallas as pl
from jax.experimental.pallas import tpu as pltpu
from jax.sharding import Mesh, PartitionSpec as P

HD = 128
VIEW = ("y", "zh")
ROW = ("zl", "x", "core")
NEAR = ("x", "core")
F32 = jnp.float32
BF16 = jnp.bfloat16
MIB = 1024 * 1024
VMEM = pl.BlockSpec(memory_space=pltpu.VMEM)
SMEM = pl.BlockSpec(memory_space=pltpu.SMEM)


def call(kernel, name, limit, out_shape, in_specs, args, hides=False, out_specs=None, scratch=()):
    return pl.pallas_call(
        kernel,
        out_shape=out_shape,
        in_specs=in_specs,
        out_specs=out_specs or jax.tree.map(lambda _: VMEM, out_shape),
        scratch_shapes=list(scratch),
        compiler_params=pltpu.CompilerParams(vmem_limit_bytes=limit * MIB),
        cost_estimate=pl.CostEstimate(
            flops=30_000_000_000 if hides else 1000, bytes_accessed=1000, transcendentals=0
        ),
        name=name,
    )(*args)


def pack_kernel(q_ref, k_ref, v_ref, out_ref, held, sems):
    heads, cols = out_ref.shape[0], q_ref.shape[0]
    copies = [
        pltpu.make_async_copy(ref, held.at[i], sems.at[i])
        for i, ref in enumerate((q_ref, k_ref, v_ref))
    ]
    for copy in copies:
        copy.start()
    for i, copy in enumerate(copies):
        copy.wait()
        for h in range(heads):
            out_ref[h, pl.ds(i * cols, cols), :] = held[i, :, pl.ds(h * HD, HD)]


def pack(query, key, value):
    cols, dim = query.shape
    shape = jax.ShapeDtypeStruct((dim // HD, 3 * cols, HD), BF16)
    return call(
        pack_kernel,
        "pack_heads",
        58,
        shape,
        [pl.BlockSpec(memory_space=pltpu.HBM)] * 3,
        (query, key, value),
        scratch=[pltpu.VMEM((3, cols, dim), BF16), pltpu.SemaphoreType.DMA((3,))],
    )


def attend_kernel(factor, step, moved_ref, extra_ref, out_ref):
    views, cols = moved_ref.shape[0], moved_ref.shape[1] // 3
    key = moved_ref[:, pl.ds(cols, cols), :].reshape(-1, HD)
    value = moved_ref[:, pl.ds(2 * cols, cols), :].reshape(-1, HD)
    for i in range(0, views, step):
        query = moved_ref[pl.ds(i, step), pl.ds(0, cols), :].reshape(-1, HD)
        scores = lax.dot_general(
            query, key, (((1,), (1,)), ((), ())), preferred_element_type=F32
        )
        top = jnp.max(scores, axis=-1, keepdims=True)
        weights = jnp.exp2((scores - top) * factor)
        total = jnp.sum(weights, axis=-1, keepdims=True)
        mixed = jnp.dot(weights.astype(BF16), value, preferred_element_type=F32) / total
        out_ref[pl.ds(i, step), pl.ds(0, cols), :] = mixed.astype(BF16).reshape(step, cols, HD)
    for i in range(views):
        out_ref[i, pl.ds(cols, extra_ref.shape[0]), :] = extra_ref[...]


def attend(moved, extra, cols):
    factor = math.log2(math.e) / math.sqrt(HD)
    shape = jax.ShapeDtypeStruct((moved.shape[0], cols + extra.shape[0], HD), BF16)
    kernel = functools.partial(attend_kernel, factor, 2)
    return call(kernel, "attend", 24, shape, [VMEM] * 2, (moved, extra), True)


def join_kernel(spot_ref, back_ref, out_ref):
    for j in range(back_ref.shape[0]):
        y, zh = lax.rem(spot_ref[2] + j // 4, 4), lax.rem(spot_ref[3] + j % 4, 4)
        out_ref[:, pl.ds(j * HD, HD)] = back_ref[y * 4 + zh, pl.ds(0, out_ref.shape[0]), :]


def join(spot, back, cols):
    shape = jax.ShapeDtypeStruct((cols, back.shape[0] * HD), BF16)
    return call(join_kernel, "join_heads", 4, shape, [SMEM, VMEM], (spot, back), True)


def mix_kernel(counts, spot_ref, left_ref, stream_ref, gain_ref, *refs):
    w_refs, (stream_out, normed_out, acc, sem) = list(refs[:-4]), refs[-4:]
    width = w_refs[0].shape[2]
    for i, count in enumerate(counts):
        core_at = spot_ref[1] if i % 2 == 0 else 1 - spot_ref[1]
        block = 2 * lax.rem(spot_ref[0] + i // 2, 4) + core_at
        at = pl.ds(pl.multiple_of(block * width, width), width)
        total, first = stream_ref[:, at].astype(F32), 0
        for w_ref in w_refs[:count]:
            weight = w_ref[...].reshape(-1, width)
            left = left_ref[:, pl.ds(first, weight.shape[0])]
            total += jnp.dot(left, weight, preferred_element_type=F32)
            first += weight.shape[0]
        acc[:, at] = total
        w_refs = w_refs[count:]
    copy = pltpu.make_async_copy(acc, stream_out, sem)
    copy.start()
    stream = acc[...]
    scale = lax.rsqrt(jnp.mean(stream * stream, axis=-1, keepdims=True) + 1e-06)
    normed_out[...] = (stream * scale * gain_ref[...]).astype(BF16)
    copy.wait()


def mix(spot, left, stream_in, gain, pieces):
    shapes = [jax.ShapeDtypeStruct(stream_in.shape, t) for t in (F32, BF16)]
    counts = [len(piece) for piece in pieces]
    flat = [array for piece in pieces for array in piece]
    args = (spot, left, stream_in, gain.reshape(1, -1), *flat)
    return call(
        functools.partial(mix_kernel, counts),
        "mix_norm",
        8,
        shapes,
        [SMEM] + [VMEM] * (len(args) - 1),
        args,
        out_specs=[pl.BlockSpec(memory_space=pltpu.HBM), VMEM],
        scratch=[pltpu.VMEM(stream_in.shape, F32), pltpu.SemaphoreType.DMA],
    )


def chip_rows(spot_ref, same, other):
    first = spot_ref[1] == 0
    same = jnp.concatenate([ref[...] for ref in same])
    other = jnp.concatenate([ref[...] for ref in other])
    return [jnp.where(first, same, other), jnp.where(first, other, same)]


def product(rows, w_ref):
    return lax.dot_general(
        jnp.concatenate(rows), w_ref[...], (((1,), (1,)), ((), ())), preferred_element_type=F32
    ).astype(BF16)


def up_most_kernel(spot_ref, *refs):
    rows_refs, (w_ref, out_ref) = refs[:-2], refs[-2:]
    rows = []
    for i in range(0, len(rows_refs), 2):
        rows += chip_rows(spot_ref, rows_refs[i : i + 1], rows_refs[i + 1 : i + 2])
    out_ref[...] = product(rows, w_ref).reshape(out_ref.shape)


def up_most(spot, rows, weight):
    shape = jax.ShapeDtypeStruct((len(rows), rows[0].shape[0], weight.shape[0]), BF16)
    args = (spot, *rows, weight)
    return call(up_most_kernel, "up_most", 14, shape, [SMEM] + [VMEM] * (len(args) - 1), args, True)


def up_last_kernel(spot_ref, *refs):
    rows_refs, (w_ref, most_ref, out_ref, edge_ref) = refs[:-4], refs[-4:]
    half = len(rows_refs) // 2
    rows = chip_rows(spot_ref, rows_refs[:half], rows_refs[half:])
    out_ref[...] = product(rows, w_ref).reshape(out_ref.shape)
    low = spot_ref[4]
    at = 2 * lax.rem(4 - low - spot_ref[0], 4) + low
    edge = most_ref[0]
    for place in range(1, 8):
        ref, index = row_of(most_ref, out_ref, place)
        edge = jnp.where(at == place, ref[index], edge)
    edge_ref[...] = edge


def row_of(most_ref, last_ref, place):
    if place in (4, 5):
        return last_ref, place - 4
    return most_ref, place if place < 4 else place - 2


def up_last(spot, rows, weight, most):
    cols, units = most.shape[1:]
    shapes = [
        jax.ShapeDtypeStruct((2, cols, units), BF16),
        jax.ShapeDtypeStruct((cols, units), BF16),
    ]
    args = (spot, *rows, weight, most)
    return call(up_last_kernel, "up_last", 8, shapes, [SMEM] + [VMEM] * (len(args) - 1), args)


def conv_kernel(offsets, spot_ref, *refs):
    most_ref, last_ref, edge_ref, taps_ref, w_ref, *outs = refs
    cols, units = edge_ref.shape
    core_at, low = spot_ref[1], spot_ref[4]
    col = lax.broadcasted_iota(jnp.int32, (cols, HD), 0)
    for n, offset in enumerate(offsets):
        x_at = lax.rem(spot_ref[0] + offset, 4)
        first_x, last_x = x_at == 0, x_at == 3
        keep_above = jnp.where(first_x & (low == 1), 0.0, 1.0)
        keep_below = jnp.where(last_x & (low == 0), 0.0, 1.0)
        places = [row_of(most_ref, last_ref, (2 * offset + k) % 8) for k in (-1, 0, 1, 2)]
        parts = [[], []]
        for u in range(0, units, HD):
            at = pl.ds(u, HD)
            edge = edge_ref[:, at].astype(F32)
            rows = [ref[index, :, at].astype(F32) for ref, index in places]
            rows[0] = jnp.where(first_x, edge, rows[0]) * keep_above
            rows[3] = jnp.where(last_x, edge, rows[3]) * keep_below
            for r in range(2):
                sums = [
                    taps_ref[pl.ds(b, 1), at] * rows[r]
                    + taps_ref[pl.ds(3 + b, 1), at] * rows[r + 1]
                    + taps_ref[pl.ds(6 + b, 1), at] * rows[r + 2]
                    for b in range(3)
                ]
                conv = (
                    sums[1]
                    + jnp.where(col == 0, 0.0, pltpu.roll(sums[0], 1, 0))
                    + jnp.where(col == cols - 1, 0.0, pltpu.roll(sums[2], cols - 1, 0))
                )
                inner = math.sqrt(2.0 / math.pi) * (conv + 0.044715 * (conv * conv * conv))
                parts[r].append((0.5 * conv * (1.0 + jnp.tanh(inner))).astype(BF16))
        active = jnp.concatenate([jnp.concatenate(p, axis=1) for p in parts], axis=0)
        out = jnp.dot(active, w_ref[...], preferred_element_type=F32)
        top, bottom = out[:cols].astype(BF16), out[cols:].astype(BF16)
        outs[2 * n][...] = jnp.where(core_at == 0, bottom, top)
        outs[2 * n + 1][...] = jnp.where(core_at == 0, top, bottom)


def conv_down(spot, offsets, most, last, edge, taps, weight, hides):
    cols = edge.shape[0]
    shape = jax.ShapeDtypeStruct((cols, weight.shape[1]), BF16)
    args = (spot, most, last, edge, taps, weight)
    return call(
        functools.partial(conv_kernel, offsets),
        "conv_gelu_down",
        14,
        [shape] * (2 * len(offsets)),
        [SMEM] + [VMEM] * (len(args) - 1),
        args,
        hides,
    )


def shift(array, axis, by):
    count = lax.axis_size(axis)
    return lax.ppermute(array, axis, [(i, (i + by) % count) for i in range(count)])


def after_all(array, *others):
    return lax.optimization_barrier((array, *others))[0]


def gather4(array, axis):
    return [array, shift(array, axis, -1), shift(array, axis, 2), shift(array, axis, 1)]


def body(
    stream_in, query_in, key_in, value_in, out_weight, norm_gain, up_weight, conv_taps, down_weight
):
    shape = stream_in.shape
    _, _, cols, dim = shape
    views = lax.axis_size(VIEW)
    near = lax.axis_size(NEAR)
    at = lax.axis_index(NEAR)
    part = up_weight.shape[1] // near
    low = 1 - lax.axis_index("zl")
    spot = jnp.stack(
        [lax.axis_index(name) for name in ("x", "core", "y", "zh")] + [low]
    ).astype(jnp.int32)
    flat = [a.reshape(cols, dim) for a in (stream_in, query_in, key_in, value_in)]

    width = dim // near
    mine = lax.dynamic_slice_in_dim(out_weight, at * width, width, 1)
    mine = jnp.stack(gather4(mine, "zh"))

    packed, strips = lax.optimization_barrier((pack(*flat[1:]), mine))
    moved = lax.all_to_all(packed, VIEW, split_axis=0, concat_axis=0, tiled=True)

    own_taps = lax.dynamic_slice_in_dim(conv_taps, at * part, part, 2).reshape(-1)
    high = lax.reduce_precision(own_taps, 8, 7)
    middle = lax.reduce_precision(own_taps - high, 8, 7)
    terms = jnp.concatenate([high, middle, own_taps - high - middle])
    term_rows = 16 * pl.cdiv(terms.size, 16 * HD)
    terms = jnp.pad(terms, (0, term_rows * HD - terms.size)).astype(BF16).reshape(term_rows, HD)
    attended = attend(moved, terms, cols)
    back = lax.all_to_all(attended, VIEW, split_axis=0, concat_axis=0, tiled=True)

    half = views // 2
    mine = jnp.concatenate(gather4(strips, "y"))
    before, after = shift(mine, "x", 1), shift(mine, "x", -1)
    across = [shift(before[:half], "x", 1), shift(after[half:], "x", -1)]
    pieces = []
    for piece in ([mine], [after], across, [before]):
        pieces += [piece, [shift(array, "core", 1) for array in piece]]

    up_slice = lax.dynamic_slice_in_dim(up_weight, at * part, part, 1).T
    down_slice = lax.dynamic_slice_in_dim(down_weight, at * part, part, 0)
    pair = after_all(jnp.concatenate([up_slice, down_slice]), mine)
    pair = lax.all_gather(pair, VIEW, axis=0, tiled=False)
    up_rows = pair[:, :part].reshape(-1, dim)

    stream, normed = mix(spot, join(spot, back, cols), flat[0], norm_gain, pieces)
    taps = back[:, cols:].reshape(views, -1)[:, : 27 * part].astype(F32)
    taps = jnp.sum(taps.reshape(views, 3, 9, part), axis=1)
    taps = taps.transpose(1, 0, 2).reshape(9, views * part)

    half = cols // 2
    before, after = shift(normed, "x", 1), shift(normed, "x", -1)
    across = [shift(before[:half], "x", 1), shift(after[half:], "x", -1)]
    rows = []
    for row in (normed, after, before):
        rows += [row, shift(row, "core", 1)]
    most = up_most(spot, rows, up_rows)
    across = [after_all(array, taps, most) for array in across]
    across += [shift(array, "core", 1) for array in across]
    last, edge_sent = up_last(spot, across, up_rows, most)
    edge = shift(edge_sent, "zl", 1)
    down_rows = after_all(pair, edge_sent)[:, part:].reshape(-1, dim)

    def add(*terms):
        return sum(term.astype(F32) for term in terms).astype(BF16)

    give, keep_2 = conv_down(spot, (2,), most, last, edge, taps, down_rows, False)
    got_2 = shift(give, "core", 1)
    give_1, keep_1, give_3, keep_3 = conv_down(
        spot, (1, 3), most, last, edge, taps, down_rows, True
    )
    got_1, got_3 = shift(give_1, "core", 1), shift(give_3, "core", 1)
    total = add(keep_2, got_2)
    last = after_all(last, total)
    give_0, keep_0 = conv_down(spot, (0,), most, last, edge, taps, down_rows, True)
    got_0 = shift(give_0, "core", 1)
    right, left = shift(total[:half], "x", 1), shift(total[half:], "x", -1)
    blank = jnp.zeros_like(left)
    right = add(keep_1, got_1, jnp.concatenate([right, blank]))
    left = add(keep_3, got_3, jnp.concatenate([blank, left]))
    right, left = shift(right, "x", 1), shift(left, "x", -1)
    result = stream
    for term in (keep_0, got_0, right, left):
        result = result + term.astype(F32)
    return result.astype(BF16).reshape(shape)


def solution(mesh):
    fine = Mesh(mesh.devices.reshape(4, 4, 2, 4, 2), ("y", "zh", "zl", "x", "core"))
    tokens = P(VIEW, ROW, None, None)
    return jax.shard_map(
        body,
        mesh=fine,
        in_specs=(
            tokens,
            tokens,
            tokens,
            tokens,
            P(VIEW, None),
            P(),
            P(None, VIEW),
            P(None, None, VIEW),
            P(VIEW, None),
        ),
        out_specs=tokens,
        check_vma=False,
    )
```

```python
import functools
import math

import jax
import jax.numpy as jnp
from jax import lax
from jax.experimental import pallas as pl
from jax.experimental.pallas import tpu as pltpu
from jax.sharding import Mesh, PartitionSpec as P

HD = 128
VIEW = ("y", "zh")
ROW = ("zl", "x", "core")
NEAR = ("x", "core")
F32 = jnp.float32
BF16 = jnp.bfloat16
MIB = 1024 * 1024
VMEM = pl.BlockSpec(memory_space=pltpu.VMEM)
SMEM = pl.BlockSpec(memory_space=pltpu.SMEM)


def call(kernel, name, limit, out_shape, in_specs, args, hides=False, out_specs=None, scratch=()):
    return pl.pallas_call(
        kernel,
        out_shape=out_shape,
        in_specs=in_specs,
        out_specs=out_specs or jax.tree.map(lambda _: VMEM, out_shape),
        scratch_shapes=list(scratch),
        compiler_params=pltpu.CompilerParams(vmem_limit_bytes=limit * MIB),
        cost_estimate=pl.CostEstimate(
            flops=30_000_000_000 if hides else 1000, bytes_accessed=1000, transcendentals=0
        ),
        name=name,
    )(*args)


def pack_kernel(q_ref, k_ref, v_ref, out_ref, held, sems):
    heads, cols = out_ref.shape[0], q_ref.shape[0]
    copies = [
        pltpu.make_async_copy(ref, held.at[i], sems.at[i])
        for i, ref in enumerate((q_ref, k_ref, v_ref))
    ]
    for copy in copies:
        copy.start()
    for i, copy in enumerate(copies):
        copy.wait()
        for h in range(heads):
            out_ref[h, pl.ds(i * cols, cols), :] = held[i, :, pl.ds(h * HD, HD)]


def pack(query, key, value):
    cols, dim = query.shape
    shape = jax.ShapeDtypeStruct((dim // HD, 3 * cols, HD), BF16)
    return call(
        pack_kernel,
        "pack_heads",
        58,
        shape,
        [pl.BlockSpec(memory_space=pltpu.HBM)] * 3,
        (query, key, value),
        scratch=[pltpu.VMEM((3, cols, dim), BF16), pltpu.SemaphoreType.DMA((3,))],
    )


def attend_kernel(factor, step, moved_ref, extra_ref, out_ref):
    views, cols = moved_ref.shape[0], moved_ref.shape[1] // 3
    key = moved_ref[:, pl.ds(cols, cols), :].reshape(-1, HD)
    value = moved_ref[:, pl.ds(2 * cols, cols), :].reshape(-1, HD)
    for i in range(0, views, step):
        query = moved_ref[pl.ds(i, step), pl.ds(0, cols), :].reshape(-1, HD)
        scores = lax.dot_general(
            query, key, (((1,), (1,)), ((), ())), preferred_element_type=F32
        )
        top = jnp.max(scores, axis=-1, keepdims=True)
        weights = jnp.exp2((scores - top) * factor)
        total = jnp.sum(weights, axis=-1, keepdims=True)
        mixed = jnp.dot(weights.astype(BF16), value, preferred_element_type=F32) / total
        out_ref[pl.ds(i, step), pl.ds(0, cols), :] = mixed.astype(BF16).reshape(step, cols, HD)
    for i in range(views):
        out_ref[i, pl.ds(cols, extra_ref.shape[0]), :] = extra_ref[...]


def attend(moved, extra, cols):
    factor = math.log2(math.e) / math.sqrt(HD)
    shape = jax.ShapeDtypeStruct((moved.shape[0], cols + extra.shape[0], HD), BF16)
    kernel = functools.partial(attend_kernel, factor, 2)
    return call(kernel, "attend", 24, shape, [VMEM] * 2, (moved, extra), True)


def join_kernel(spot_ref, back_ref, out_ref):
    for j in range(back_ref.shape[0]):
        y, zh = lax.rem(spot_ref[2] + j // 4, 4), lax.rem(spot_ref[3] + j % 4, 4)
        out_ref[:, pl.ds(j * HD, HD)] = back_ref[y * 4 + zh, pl.ds(0, out_ref.shape[0]), :]


def join(spot, back, cols):
    shape = jax.ShapeDtypeStruct((cols, back.shape[0] * HD), BF16)
    return call(join_kernel, "join_heads", 4, shape, [SMEM, VMEM], (spot, back), True)


def mix_kernel(counts, spot_ref, left_ref, stream_ref, gain_ref, *refs):
    w_refs, (stream_out, normed_out, acc, sem) = list(refs[:-4]), refs[-4:]
    width = w_refs[0].shape[2]
    for i, count in enumerate(counts):
        core_at = spot_ref[1] if i % 2 == 0 else 1 - spot_ref[1]
        block = 2 * lax.rem(spot_ref[0] + i // 2, 4) + core_at
        at = pl.ds(pl.multiple_of(block * width, width), width)
        total, first = stream_ref[:, at].astype(F32), 0
        for w_ref in w_refs[:count]:
            weight = w_ref[...].reshape(-1, width)
            left = left_ref[:, pl.ds(first, weight.shape[0])]
            total += jnp.dot(left, weight, preferred_element_type=F32)
            first += weight.shape[0]
        acc[:, at] = total
        w_refs = w_refs[count:]
    copy = pltpu.make_async_copy(acc, stream_out, sem)
    copy.start()
    stream = acc[...]
    scale = lax.rsqrt(jnp.mean(stream * stream, axis=-1, keepdims=True) + 1e-06)
    normed_out[...] = (stream * scale * gain_ref[...]).astype(BF16)
    copy.wait()


def mix(spot, left, stream_in, gain, pieces):
    shapes = [jax.ShapeDtypeStruct(stream_in.shape, t) for t in (F32, BF16)]
    counts = [len(piece) for piece in pieces]
    flat = [array for piece in pieces for array in piece]
    args = (spot, left, stream_in, gain.reshape(1, -1), *flat)
    return call(
        functools.partial(mix_kernel, counts),
        "mix_norm",
        8,
        shapes,
        [SMEM] + [VMEM] * (len(args) - 1),
        args,
        out_specs=[pl.BlockSpec(memory_space=pltpu.HBM), VMEM],
        scratch=[pltpu.VMEM(stream_in.shape, F32), pltpu.SemaphoreType.DMA],
    )


def chip_rows(spot_ref, same, other):
    first = spot_ref[1] == 0
    same = jnp.concatenate([ref[...] for ref in same])
    other = jnp.concatenate([ref[...] for ref in other])
    return [jnp.where(first, same, other), jnp.where(first, other, same)]


def product(rows, w_ref):
    return lax.dot_general(
        jnp.concatenate(rows), w_ref[...], (((1,), (1,)), ((), ())), preferred_element_type=F32
    ).astype(BF16)


def up_most_kernel(spot_ref, *refs):
    rows_refs, (w_ref, out_ref) = refs[:-2], refs[-2:]
    rows = []
    for i in range(0, len(rows_refs), 2):
        rows += chip_rows(spot_ref, rows_refs[i : i + 1], rows_refs[i + 1 : i + 2])
    out_ref[...] = product(rows, w_ref).reshape(out_ref.shape)


def up_most(spot, rows, weight):
    shape = jax.ShapeDtypeStruct((len(rows), rows[0].shape[0], weight.shape[0]), BF16)
    args = (spot, *rows, weight)
    return call(up_most_kernel, "up_most", 14, shape, [SMEM] + [VMEM] * (len(args) - 1), args, True)


def up_last_kernel(spot_ref, *refs):
    rows_refs, (w_ref, most_ref, out_ref, edge_ref) = refs[:-4], refs[-4:]
    half = len(rows_refs) // 2
    rows = chip_rows(spot_ref, rows_refs[:half], rows_refs[half:])
    out_ref[...] = product(rows, w_ref).reshape(out_ref.shape)
    low = spot_ref[4]
    at = 2 * lax.rem(4 - low - spot_ref[0], 4) + low
    edge = most_ref[0]
    for place in range(1, 8):
        ref, index = row_of(most_ref, out_ref, place)
        edge = jnp.where(at == place, ref[index], edge)
    edge_ref[...] = edge


def row_of(most_ref, last_ref, place):
    if place in (4, 5):
        return last_ref, place - 4
    return most_ref, place if place < 4 else place - 2


def up_last(spot, rows, weight, most):
    cols, units = most.shape[1:]
    shapes = [
        jax.ShapeDtypeStruct((2, cols, units), BF16),
        jax.ShapeDtypeStruct((cols, units), BF16),
    ]
    args = (spot, *rows, weight, most)
    return call(up_last_kernel, "up_last", 8, shapes, [SMEM] + [VMEM] * (len(args) - 1), args)


def conv_kernel(offsets, spot_ref, *refs):
    most_ref, last_ref, edge_ref, taps_ref, w_ref, *outs = refs
    cols, units = edge_ref.shape
    core_at, low = spot_ref[1], spot_ref[4]
    col = lax.broadcasted_iota(jnp.int32, (cols, HD), 0)
    for n, offset in enumerate(offsets):
        x_at = lax.rem(spot_ref[0] + offset, 4)
        first_x, last_x = x_at == 0, x_at == 3
        keep_above = jnp.where(first_x & (low == 1), 0.0, 1.0)
        keep_below = jnp.where(last_x & (low == 0), 0.0, 1.0)
        places = [row_of(most_ref, last_ref, (2 * offset + k) % 8) for k in (-1, 0, 1, 2)]
        parts = [[], []]
        for u in range(0, units, HD):
            at = pl.ds(u, HD)
            edge = edge_ref[:, at].astype(F32)
            rows = [ref[index, :, at].astype(F32) for ref, index in places]
            rows[0] = jnp.where(first_x, edge, rows[0]) * keep_above
            rows[3] = jnp.where(last_x, edge, rows[3]) * keep_below
            for r in range(2):
                sums = [
                    taps_ref[pl.ds(b, 1), at] * rows[r]
                    + taps_ref[pl.ds(3 + b, 1), at] * rows[r + 1]
                    + taps_ref[pl.ds(6 + b, 1), at] * rows[r + 2]
                    for b in range(3)
                ]
                conv = (
                    sums[1]
                    + jnp.where(col == 0, 0.0, pltpu.roll(sums[0], 1, 0))
                    + jnp.where(col == cols - 1, 0.0, pltpu.roll(sums[2], cols - 1, 0))
                )
                inner = math.sqrt(2.0 / math.pi) * (conv + 0.044715 * (conv * conv * conv))
                parts[r].append((0.5 * conv * (1.0 + jnp.tanh(inner))).astype(BF16))
        active = jnp.concatenate([jnp.concatenate(p, axis=1) for p in parts], axis=0)
        out = jnp.dot(active, w_ref[...], preferred_element_type=F32)
        top, bottom = out[:cols].astype(BF16), out[cols:].astype(BF16)
        outs[2 * n][...] = jnp.where(core_at == 0, bottom, top)
        outs[2 * n + 1][...] = jnp.where(core_at == 0, top, bottom)


def conv_down(spot, offsets, most, last, edge, taps, weight, hides):
    cols = edge.shape[0]
    shape = jax.ShapeDtypeStruct((cols, weight.shape[1]), BF16)
    args = (spot, most, last, edge, taps, weight)
    return call(
        functools.partial(conv_kernel, offsets),
        "conv_gelu_down",
        14,
        [shape] * (2 * len(offsets)),
        [SMEM] + [VMEM] * (len(args) - 1),
        args,
        hides,
    )


def shift(array, axis, by):
    count = lax.axis_size(axis)
    return lax.ppermute(array, axis, [(i, (i + by) % count) for i in range(count)])


def after_all(array, *others):
    return lax.optimization_barrier((array, *others))[0]


def gather4(array, axis):
    return [array, shift(array, axis, -1), shift(array, axis, 2), shift(array, axis, 1)]


def body(
    stream_in, query_in, key_in, value_in, out_weight, norm_gain, up_weight, conv_taps, down_weight
):
    shape = stream_in.shape
    _, _, cols, dim = shape
    views = lax.axis_size(VIEW)
    near = lax.axis_size(NEAR)
    at = lax.axis_index(NEAR)
    part = up_weight.shape[1] // near
    low = 1 - lax.axis_index("zl")
    spot = jnp.stack(
        [lax.axis_index(name) for name in ("x", "core", "y", "zh")] + [low]
    ).astype(jnp.int32)
    flat = [a.reshape(cols, dim) for a in (stream_in, query_in, key_in, value_in)]

    width = dim // near
    mine = lax.dynamic_slice_in_dim(out_weight, at * width, width, 1)
    mine = jnp.stack(gather4(mine, "zh"))

    packed, strips = lax.optimization_barrier((pack(*flat[1:]), mine))
    moved = lax.all_to_all(packed, VIEW, split_axis=0, concat_axis=0, tiled=True)

    own_taps = lax.dynamic_slice_in_dim(conv_taps, at * part, part, 2).reshape(-1)
    high = lax.reduce_precision(own_taps, 8, 7)
    middle = lax.reduce_precision(own_taps - high, 8, 7)
    terms = jnp.concatenate([high, middle, own_taps - high - middle])
    term_rows = 16 * pl.cdiv(terms.size, 16 * HD)
    terms = jnp.pad(terms, (0, term_rows * HD - terms.size)).astype(BF16).reshape(term_rows, HD)
    attended = attend(moved, terms, cols)
    back = lax.all_to_all(attended, VIEW, split_axis=0, concat_axis=0, tiled=True)

    half = views // 2
    round_y = gather4(strips, "y")
    mine = jnp.concatenate(round_y)
    before, after = shift(mine, "x", 1), shift(mine, "x", -1)
    across = [shift(before[:half], "x", 1), shift(after[half:], "x", -1)]
    pieces = []
    for piece in ([mine], [after], across, [before]):
        pieces += [piece, [shift(array, "core", 1) for array in piece]]

    up_slice = lax.dynamic_slice_in_dim(up_weight, at * part, part, 1).T
    down_slice = lax.dynamic_slice_in_dim(down_weight, at * part, part, 0)
    pair = after_all(jnp.concatenate([up_slice, down_slice]), round_y[1])
    pair = lax.all_gather(pair, VIEW, axis=0, tiled=False)
    up_rows = pair[:, :part].reshape(-1, dim)

    stream, normed = mix(spot, join(spot, back, cols), flat[0], norm_gain, pieces)
    taps = back[:, cols:].reshape(views, -1)[:, : 27 * part].astype(F32)
    taps = jnp.sum(taps.reshape(views, 3, 9, part), axis=1)
    taps = taps.transpose(1, 0, 2).reshape(9, views * part)

    half = cols // 2
    before, after = shift(normed, "x", 1), shift(normed, "x", -1)
    across = [shift(before[:half], "x", 1), shift(after[half:], "x", -1)]
    rows = []
    for row in (normed, after, before):
        rows += [row, shift(row, "core", 1)]
    most = up_most(spot, rows, up_rows)
    across = [after_all(array, taps, most) for array in across]
    across += [shift(array, "core", 1) for array in across]
    last, edge_sent = up_last(spot, across, up_rows, most)
    edge = shift(edge_sent, "zl", 1)
    down_rows = after_all(pair, edge_sent)[:, part:].reshape(-1, dim)

    def add(*terms):
        return sum(term.astype(F32) for term in terms).astype(BF16)

    give, keep_2 = conv_down(spot, (2,), most, last, edge, taps, down_rows, False)
    got_2 = shift(give, "core", 1)
    give_1, keep_1, give_3, keep_3, give_0, keep_0 = conv_down(
        spot, (1, 3, 0), most, last, edge, taps, down_rows, True
    )
    got_1, got_3, got_0 = (shift(give, "core", 1) for give in (give_1, give_3, give_0))
    total = add(keep_2, got_2)
    right, left = shift(total[:half], "x", 1), shift(total[half:], "x", -1)
    blank = jnp.zeros_like(left)
    right = add(keep_1, got_1, jnp.concatenate([right, blank]))
    left = add(keep_3, got_3, jnp.concatenate([blank, left]))
    right, left = shift(right, "x", 1), shift(left, "x", -1)
    result = stream
    for term in (keep_0, got_0, right, left):
        result = result + term.astype(F32)
    return result.astype(BF16).reshape(shape)


def solution(mesh):
    fine = Mesh(mesh.devices.reshape(4, 4, 2, 4, 2), ("y", "zh", "zl", "x", "core"))
    tokens = P(VIEW, ROW, None, None)
    return jax.shard_map(
        body,
        mesh=fine,
        in_specs=(
            tokens,
            tokens,
            tokens,
            tokens,
            P(VIEW, None),
            P(),
            P(None, VIEW),
            P(None, None, VIEW),
            P(VIEW, None),
        ),
        out_specs=tokens,
        check_vma=False,
    )
```
